128 devices in a mesh: gx: 16 (over z, y), gy: 8 (over x, core).
Axes of the slice: x: 4, y: 4, z: 4, core: 2. Of those that a mesh axis runs over, the one named last changes fastest.
Arguments:
- owner_list: int32 [128, 128], replicated, may hold values from 0 to 128, as said below
- ice_mask: int32 [14336, 256], P(('gx', 'gy')), may hold values 0 or 1
- velocity: float32 [14336, 2, 256], P(('gx', 'gy')), may hold values from -2 to 2
- stress: float32 [14336, 3, 256], P(('gx', 'gy')), may hold values from -2 to 2
- thickness: float32 [14336, 5, 256], P(('gx', 'gy')), may hold values from 0.3 to 1.5
- concentration: float32 [14336, 5, 256], P(('gx', 'gy')), may hold values from 0.19 to 0.2
- ocean_u: float32 [2048, 2048], P('gy', 'gx'), may hold values from -3 to 3
- ocean_v: float32 [2048, 2048], P('gy', 'gx'), may hold values from -3 to 3
- wind_x: float32 [2048, 2048], P('gy', 'gx'), may hold values from -3 to 3
- wind_y: float32 [2048, 2048], P('gy', 'gx'), may hold values from -3 to 3
- surface_temp: float32 [2048, 2048], P('gy', 'gx'), may hold values from -4 to 4
Outputs:
- velocity_out: float32 [14336, 2, 256], P(('gx', 'gy'))
- stress_out: float32 [14336, 3, 256], P(('gx', 'gy'))
- ocean_drag: float32 [2, 2048, 2048], P(None, 'gy', 'gx')
The draws below stay inside these ranges and needn't reach their ends.
Inputs may be any that keep to these rules, and one draw needn't show every extreme that they name: owner_list[s, k] is the owning device (linear index over gx then gy) of block k of ocean tile s, or the device count if the block holds no ice. Every device owns exactly 112 blocks; no tile has more than 2 blocks owned by one device, and some tile has exactly 2 owned by some device.
All inputs are finite; a program needn't handle non-finite values. No bound on the sum of `ice_mask` on one device may be relied on, other than what follows from the above.
Results may differ from the reference program's by a relative error of at most 0.00002.
Values sent between devices are 32-bit elements; how exact they have to be, the bound alone decides.
No kernel may reach another device: no remote copies, remote signals or barrier semaphores. Data moves between devices by JAX's collectives and lax.ppermute only.
A program may use at most 128 MiB of HBM per device.

```python
import jax
import jax.numpy as jnp
from jax import lax

NCAT = 5
BROWS = 8
BCOLS = 32
BPT = 128
SUBS = 8
TLON = 128
TLAT = 256
NLAT = 2048
NLON = 2048
SLOTS = 112
ICEBLK = 14336
N_GX = 16
N_GY = 8
DEVICES = 128


def draw_owner_list(key, part):
    key = jax.random.fold_in(key, 11)
    capacity = max(2, 2 * BPT // DEVICES)
    block_total = DEVICES * BPT
    tile_index = jnp.arange(block_total, dtype=jnp.int32) // BPT
    lat_row = tile_index % N_GY
    polar_rank = jnp.abs(2 * lat_row - (N_GY - 1))
    key_jitter, key_full = jax.random.split(key)
    jitter = jax.random.randint(key_jitter, (block_total,), 0, 1024, dtype=jnp.int32)
    full_tile = jax.random.randint(key_full, (), 0, DEVICES, dtype=jnp.int32)
    priority = jnp.where(tile_index == full_tile, 64, polar_rank)
    scores = (priority * DEVICES + tile_index) * 1024 + jitter
    ordering = jnp.argsort(-scores, stable=True)
    position = jnp.zeros((block_total,), jnp.int32).at[ordering].set(jnp.arange(block_total, dtype=jnp.int32))
    icy_flag = (position < SLOTS * DEVICES).astype(jnp.int32)
    ranked = position // capacity
    owners = jnp.where(icy_flag > 0, ranked % DEVICES, DEVICES)
    return owners.reshape(DEVICES, BPT).astype(jnp.int32)


def plant(entries, stream_key, smallest, largest):
    longest = entries.shape.index(max(entries.shape))
    spots = []
    for shift in (0, 1):
        where = [jax.random.randint(jax.random.fold_in(stream_key, axis), (), 0, length) for axis, length in enumerate(entries.shape)]
        where[longest] = (where[longest] + shift) % entries.shape[longest]
        spots.append(tuple(where))
    return entries.at[spots[0]].set(smallest).at[spots[1]].set(largest)


def block_scale(rng, shape, shards, low, top_value):
    factor_of = 1.0
    for axis_at, blocks in shards:
        draws = jax.random.uniform(jax.random.fold_in(jax.random.fold_in(rng, 6), axis_at), (blocks,), jnp.float32, low / len(shards), top_value / len(shards))
        factor_of = factor_of * jnp.repeat(jnp.exp(draws), shape[axis_at] // blocks).reshape((-1,) + (1,) * (len(shape) - 1 - axis_at))
    return factor_of


def bell_draw(own_key, extent, spread, reach, pieces=(), kind=jnp.bfloat16):
    level = block_scale(own_key, extent, pieces, -0.22, 0.18) if pieces else 1.0
    result = jax.random.normal(own_key, extent, jnp.float32) * spread * level
    return jnp.minimum(jnp.maximum(result, -reach), reach).astype(kind)


def setup_inputs(seed: int = 0) -> dict:
    arg_keys = jax.random.split(jax.random.key(seed), 12)
    return {
        "owner_list": draw_owner_list(jax.random.fold_in(arg_keys[11], 71), 0),
        "ice_mask": plant((jax.random.randint(arg_keys[1], (ICEBLK, BROWS * BCOLS), 0, 8) < 7).astype(jnp.int32), jax.random.fold_in(arg_keys[1], 1), 0, 1),
        "velocity": bell_draw(arg_keys[2], (ICEBLK, 2, BROWS * BCOLS), 0.3, 2.0, ((0, 128),), jnp.float32),
        "stress": bell_draw(arg_keys[3], (ICEBLK, 3, BROWS * BCOLS), 0.3, 2.0, ((0, 128),), jnp.float32),
        "thickness": jnp.clip(0.3 + 1.2 * jax.random.uniform(arg_keys[4], (ICEBLK, NCAT, BROWS * BCOLS), jnp.float32) ** block_scale(arg_keys[4], (ICEBLK, NCAT, BROWS * BCOLS), ((0, 128),), -0.2, 0.2), 0.3, 1.5),
        "concentration": jnp.clip(0.19 + 0.010000005 * jax.random.uniform(arg_keys[5], (ICEBLK, NCAT, BROWS * BCOLS), jnp.float32) ** block_scale(arg_keys[5], (ICEBLK, NCAT, BROWS * BCOLS), ((0, 128),), -0.2, 0.2), 0.19, 0.2),
        "ocean_u": bell_draw(arg_keys[6], (NLAT, NLON), 0.5, 3.0, ((0, 8), (1, 16)), jnp.float32),
        "ocean_v": bell_draw(arg_keys[7], (NLAT, NLON), 0.5, 3.0, ((0, 8), (1, 16)), jnp.float32),
        "wind_x": bell_draw(arg_keys[8], (NLAT, NLON), 0.5, 3.0, ((0, 8), (1, 16)), jnp.float32),
        "wind_y": bell_draw(arg_keys[9], (NLAT, NLON), 0.5, 3.0, ((0, 8), (1, 16)), jnp.float32),
        "surface_temp": bell_draw(arg_keys[10], (NLAT, NLON), 1.0, 4.0, ((0, 8), (1, 16)), jnp.float32),
    }


PSTAR = 1.0
CSTAR = 20.0
MELT_RATE = 0.5
ECCEN = 2.0
DELTA_MIN = 0.1
RELAX = 0.4
DT_ELASTIC = 0.5
DRAG_COEF = 1.0
FCOR = 1.0
SPEED_FLOOR = 0.01

def grid_shift(values, drow, dcol):
    padded = jnp.pad(values, [(0, 0)] * (values.ndim - 2) + [(1, 1), (1, 1)])
    return padded[..., 1 + drow:1 + drow + values.shape[-2], 1 + dcol:1 + dcol + values.shape[-1]]

def subcycle(state_in, forcing, shifter):
    east_vel, north_vel, sig_sum, sig_diff, sig_shear = state_in
    ocean_east, ocean_north, wind_east, wind_north, coriolis, strength, ice_mass, cover = forcing
    strain_xx = 0.5 * (shifter(east_vel, 0, 1) - shifter(east_vel, 0, -1))
    strain_yy = 0.5 * (shifter(north_vel, 1, 0) - shifter(north_vel, -1, 0))
    shear_rate = 0.5 * (shifter(east_vel, 1, 0) - shifter(east_vel, -1, 0) + shifter(north_vel, 0, 1) - shifter(north_vel, 0, -1))
    divergence = strain_xx + strain_yy
    tension = strain_xx - strain_yy
    deformation = jnp.sqrt(divergence * divergence + (tension * tension + shear_rate * shear_rate) / (ECCEN * ECCEN) + DELTA_MIN * DELTA_MIN)
    pressure_ratio = strength / deformation
    sig_sum = cover * (sig_sum + RELAX * pressure_ratio * (divergence - deformation)) / (1.0 + RELAX)
    sig_diff = cover * (sig_diff + RELAX * pressure_ratio * tension / (ECCEN * ECCEN)) / (1.0 + RELAX)
    sig_shear = cover * (sig_shear + RELAX * pressure_ratio * shear_rate / (2.0 * ECCEN * ECCEN)) / (1.0 + RELAX)
    sig_xx = 0.5 * (sig_sum + sig_diff)
    sig_yy = 0.5 * (sig_sum - sig_diff)
    force_east = 0.5 * (shifter(sig_xx, 0, 1) - shifter(sig_xx, 0, -1)) + 0.5 * (shifter(sig_shear, 1, 0) - shifter(sig_shear, -1, 0))
    force_north = 0.5 * (shifter(sig_shear, 0, 1) - shifter(sig_shear, 0, -1)) + 0.5 * (shifter(sig_yy, 1, 0) - shifter(sig_yy, -1, 0))
    drag_now = DRAG_COEF * jnp.sqrt((ocean_east - east_vel) ** 2 + (ocean_north - north_vel) ** 2 + SPEED_FLOOR)
    inertia = ice_mass / DT_ELASTIC
    diagonal = inertia + drag_now
    coriolis_term = ice_mass * coriolis
    rhs_east = inertia * east_vel + force_east + wind_east + drag_now * ocean_east
    rhs_north = inertia * north_vel + force_north + wind_north + drag_now * ocean_north
    determinant = diagonal * diagonal + coriolis_term * coriolis_term
    east_vel = cover * (diagonal * rhs_east + coriolis_term * rhs_north) / determinant
    north_vel = cover * (diagonal * rhs_north - coriolis_term * rhs_east) / determinant
    return (east_vel, north_vel, sig_sum, sig_diff, sig_shear)

def drag_stress(east_vel, north_vel, ocean_east, ocean_north, cover, stack_axis):
    drag_now = DRAG_COEF * jnp.sqrt((ocean_east - east_vel) ** 2 + (ocean_north - north_vel) ** 2 + SPEED_FLOOR)
    return jnp.stack([cover * drag_now * (east_vel - ocean_east), cover * drag_now * (north_vel - ocean_north)], axis=stack_axis)

def blocks_to_grid(blocks):
    fields = blocks.shape[1]
    shaped = blocks.reshape(N_GX, N_GY, TLAT // BROWS, TLON // BCOLS, fields, BROWS, BCOLS)
    return shaped.transpose(4, 1, 2, 5, 0, 3, 6).reshape(fields, NLAT, NLON)

def grid_to_blocks(grid):
    fields = grid.shape[0]
    shaped = grid.reshape(fields, N_GY, TLAT // BROWS, BROWS, N_GX, TLON // BCOLS, BCOLS)
    return shaped.transpose(4, 1, 2, 5, 0, 3, 6).reshape(DEVICES * BPT, fields, BROWS * BCOLS)

def ice_rows(owner_list):
    flattened = owner_list.reshape(-1).astype(jnp.int32)
    onehot = (flattened[:, None] == jnp.arange(DEVICES + 1, dtype=jnp.int32)[None, :]).astype(jnp.int32)
    earlier = jnp.cumsum(onehot, axis=0) - onehot
    position = lax.optimization_barrier(jnp.sum(earlier * onehot, axis=1))
    return (flattened * SLOTS + position).astype(jnp.int32)

def reference(owner_list, ice_mask, velocity, stress, thickness, concentration, ocean_u, ocean_v, wind_x, wind_y, surface_temp):
    ice_index = ice_rows(owner_list)
    cover_ice = ice_mask.astype(jnp.float32)[:, None, :]
    conc_total = lax.optimization_barrier(jnp.sum(concentration, axis=1, keepdims=True))
    mass_ice = lax.optimization_barrier(jnp.sum(thickness * concentration, axis=1, keepdims=True))
    strength_raw = PSTAR * mass_ice * jnp.exp(-CSTAR * (1.0 - conc_total))
    packed = jnp.concatenate([velocity, stress, strength_raw, mass_ice, cover_ice], axis=1)
    gridded = blocks_to_grid(jnp.take(packed, ice_index, axis=0, mode='fill', fill_value=0.0))
    melt_factor = jnp.exp(-MELT_RATE * jnp.maximum(surface_temp, 0.0))
    lat_index = jnp.arange(NLAT).astype(jnp.float32)
    coriolis = jnp.broadcast_to((FCOR * (2.0 * (lat_index + 0.5) / NLAT - 1.0))[:, None], (NLAT, NLON))
    forcing = (ocean_u, ocean_v, wind_x, wind_y, coriolis, gridded[5] * melt_factor, gridded[6], gridded[7])
    state_now = tuple((gridded[member] for member in range(5)))
    for substep in range(SUBS):
        state_now = subcycle(state_now, forcing, grid_shift)
    ocean_drag = drag_stress(state_now[0], state_now[1], ocean_u, ocean_v, gridded[7], 0)
    final_blocks = grid_to_blocks(jnp.stack(state_now))
    final_ice = jnp.zeros((ICEBLK, 5, BROWS * BCOLS), jnp.float32).at[ice_index].set(final_blocks, mode='drop')
    return (final_ice[:, :2], final_ice[:, 2:], ocean_drag)
```

```python
import jax
import jax.numpy as jnp
from jax import lax
from jax.experimental import pallas as pl
from jax.experimental.pallas import tpu as pltpu
from jax.sharding import PartitionSpec as P

AXES = ("gx", "gy")
TILES = 128
SLOTS = 112
ROWS = 256
LANES = 128
BANDS = ROWS // 8
HALO = 16
SUBS = 8
FIELDS = 8
FINAL = 5
I14 = 1.0 / 1.4
F32 = jnp.float32
VMEM_BYTES = 24 * 1024 * 1024


def lane_ids(rows=8):
    return lax.broadcasted_iota(jnp.int32, (rows, LANES), 1)


def roll(x, shift):
    return pltpu.roll(x, shift % LANES, 1)


def swap_chunks(four):
    lane = lane_ids(four[0].shape[0])
    low = lane < 64
    a, b, c, d = four
    a, c = jnp.where(low, a, roll(c, 64)), jnp.where(low, roll(a, 64), c)
    b, d = jnp.where(low, b, roll(d, 64)), jnp.where(low, roll(b, 64), d)
    even = (lane & 32) == 0
    a, b = jnp.where(even, a, roll(b, 32)), jnp.where(even, roll(a, 96), b)
    c, d = jnp.where(even, c, roll(d, 32)), jnp.where(even, roll(c, 96), d)
    return [a, b, c, d]


def pack_ice_kernel(
    owner_ref, mask_ref, vel_ref, str_ref, thk_ref, con_ref, out_ref, starts_ref, pos_ref, blk, near, sem
):
    me = lax.axis_index("gx") * lax.axis_size("gy") + lax.axis_index("gy")
    first = lax.broadcasted_iota(jnp.int32, (TILES, TILES), 0)
    second = lax.broadcasted_iota(jnp.int32, (TILES, TILES), 1)
    before = jnp.where(first < second, 1.0, 0.0)
    ones = jnp.ones((8, TILES), F32)
    owned = jnp.where(owner_ref[...] == me, 1.0, 0.0)
    counts = lax.dot_general(ones, owned, (((1,), (1,)), ((), ())), preferred_element_type=F32)
    starts = jnp.dot(counts, before, preferred_element_type=F32)
    starts_ref[...] = starts.astype(jnp.int32)
    copy = pltpu.make_async_copy(starts_ref, near, sem)
    copy.start()

    mine = jnp.broadcast_to(owner_ref[pl.ds(me, 1), :], (TILES, TILES)).astype(F32)
    twin = jnp.where(mine.T == mine, before, 0.0)
    rank = jnp.dot(ones, twin, preferred_element_type=F32)
    mine = mine[:8]
    pos_ref[...] = jnp.where(mine < TILES, 2.0 * mine + rank, -1.0).astype(jnp.int32)

    def block(i):
        con = con_ref[i]
        mass = jnp.sum(thk_ref[i] * con, axis=0, keepdims=True)
        total = jnp.sum(con, axis=0, keepdims=True)
        strength = mass * jnp.exp(-20.0 * (1.0 - total))
        cover = mask_ref[pl.ds(i, 1), :].astype(F32)
        for h in range(2):
            cut = slice(h * LANES, (h + 1) * LANES)
            at = h * FIELDS
            blk[i, at : at + 2, :] = vel_ref[i, :, cut]
            blk[i, at + 2 : at + 5, :] = str_ref[i, :, cut]
            blk[i, at + 5 : at + 6, :] = strength[:, cut]
            blk[i, at + 6 : at + 7, :] = mass[:, cut]
            blk[i, at + 7 : at + 8, :] = cover[:, cut]

    def some(g, carry):
        for j in range(8):
            block(g * 8 + j)
        return carry

    lax.fori_loop(0, SLOTS // 8, some, 0)
    copy.wait()
    for t in range(TILES):
        start = near[0, t]
        out_ref[2 * t] = blk[start]
        out_ref[2 * t + 1] = blk[start + 1]


def pack_ice(owner_list, ice_mask, velocity, stress, thickness, concentration):
    return pl.pallas_call(
        pack_ice_kernel,
        out_shape=(
            jax.ShapeDtypeStruct((2 * TILES, 2 * FIELDS, LANES), F32),
            jax.ShapeDtypeStruct((8, TILES), jnp.int32),
            jax.ShapeDtypeStruct((8, TILES), jnp.int32),
        ),
        scratch_shapes=[
            pltpu.VMEM((SLOTS + 8, 2 * FIELDS, LANES), F32),
            pltpu.SMEM((8, TILES), jnp.int32),
            pltpu.SemaphoreType.DMA(()),
        ],
        compiler_params=pltpu.CompilerParams(vmem_limit_bytes=VMEM_BYTES),
        name="pack_ice",
    )(owner_list, ice_mask, velocity, stress, thickness, concentration)


def ocean_edges_kernel(ou_ref, ov_ref, wx_ref, wy_ref, out_ref):
    lane = lane_ids()
    for i in range(BANDS):
        rows = slice(8 * i, 8 * i + 8)
        total = jnp.zeros((8, LANES), F32)
        for f, ref in enumerate((ou_ref, ov_ref, wx_ref, wy_ref)):
            x = ref[rows, :]
            total = jnp.where(lane // HALO == f, roll(x, f * HALO), total)
            total = jnp.where(lane // HALO == f + 4, roll(x, (f + 5) * HALO), total)
        out_ref[rows, :] = total


def ocean_edges(ou, ov, wx, wy):
    return pl.pallas_call(
        ocean_edges_kernel,
        out_shape=jax.ShapeDtypeStruct((ROWS, LANES), F32),
        name="ocean_edges",
    )(ou, ov, wx, wy)


def unpack_tile_kernel(pos_ref, recv_ref, temp_ref, tile_ref, west_ref, east_ref):
    lane = lane_ids()

    def band(i, carry):
        base = pl.multiple_of(i * 64, 64)
        row = pl.multiple_of(i * 8, 8)
        for h in range(2):
            four = []
            for c in range(4):
                pos = pos_ref[0, i * 4 + c]
                got = recv_ref[jnp.maximum(pos, 0), h * FIELDS : (h + 1) * FIELDS, :]
                four.append(jnp.where(pos >= 0, got, 0.0))
            for r, x in enumerate(swap_chunks(four)):
                tile_ref[pl.ds(base + h * 4 + r, FIELDS, stride=8), :] = x
        melt = jnp.exp(-0.5 * jnp.maximum(temp_ref[pl.ds(row, 8), :], 0.0))
        at = pl.multiple_of(base + 40, 8)
        tile_ref[pl.ds(at, 8), :] = tile_ref[pl.ds(at, 8), :] * melt
        west = jnp.zeros((8, LANES), F32)
        east = jnp.zeros((8, LANES), F32)
        for f in range(FIELDS):
            x = tile_ref[pl.ds(pl.multiple_of(base + f * 8, 8), 8), :]
            here = lane // HALO == f
            west = jnp.where(here, roll(x, f * HALO), west)
            east = jnp.where(here, roll(x, (f + 1) * HALO), east)
        west_ref[pl.ds(row, 8), :] = west
        east_ref[pl.ds(row, 8), :] = east
        return carry

    lax.fori_loop(0, BANDS, band, 0)


def unpack_tile(pos, recv, temp):
    return pl.pallas_call(
        unpack_tile_kernel,
        in_specs=[
            pl.BlockSpec(memory_space=pltpu.SMEM),
            pl.BlockSpec(memory_space=pltpu.VMEM),
            pl.BlockSpec(memory_space=pltpu.VMEM),
        ],
        out_shape=(
            jax.ShapeDtypeStruct((BANDS * FIELDS * 8, LANES), F32),
            jax.ShapeDtypeStruct((ROWS, LANES), F32),
            jax.ShapeDtypeStruct((ROWS, LANES), F32),
        ),
        compiler_params=pltpu.CompilerParams(vmem_limit_bytes=VMEM_BYTES),
        name="unpack_tile",
    )(pos, recv, temp)


STATE = ("u", "v", "p", "m", "t")
STATIC = ("ou", "ov", "wx", "wy", "inertia", "turn", "k", "cover")


def put_ice(s, i, ice, row_ids, grid_rows):
    u, v, total, diff, shear, strength, mass, cover = ice
    at = slice(8 + 8 * i, 16 + 8 * i)
    here = slice(8 * i, 8 * i + 8)
    s["u"][at, :] = u
    s["v"][at, :] = v
    s["p"][at, :] = cover * (total + diff)
    s["m"][at, :] = cover * (total - diff)
    s["t"][at, :] = cover * (shear + shear)
    coriolis = 2.0 * (row_ids.astype(F32) + 0.5) / grid_rows - 1.0
    s["inertia"][here, :] = 2.0 * mass
    s["turn"][here, :] = mass * coriolis
    s["k"][here, :] = (0.4 * I14) * (cover * strength)
    s["cover"][here, :] = cover


def put_ocean(s, i, ocean):
    here = slice(8 * i, 8 * i + 8)
    for name, x in zip(("ou", "ov", "wx", "wy"), ocean):
        s[name][here, :] = x


def clear_ends(s, chunks):
    zero = jnp.zeros((8, LANES), F32)
    for name in STATE:
        s[name][0:8, :] = zero
        s[name][8 + 8 * chunks : 16 + 8 * chunks, :] = zero


def run_subcycles(s, chunks):
    def subcycle(step, carry):
        for i in range(chunks):
            a = 8 + 8 * i
            at, up, down = slice(a, a + 8), slice(a + 1, a + 9), slice(a - 1, a + 7)
            here = slice(8 * i, 8 * i + 8)
            u, v = s["u"][at, :], s["v"][at, :]
            exx = roll(u, -1) - roll(u, 1)
            eyy = s["v"][up, :] - s["v"][down, :]
            shear = (s["u"][up, :] - s["u"][down, :]) + (roll(v, -1) - roll(v, 1))
            div = exx + eyy
            ten = exx - eyy
            q = div * div + 0.25 * (ten * ten + shear * shear) + 0.04
            inv = lax.rsqrt(q)
            k = s["k"][here, :] * inv
            base = div - q * inv
            ten = 0.25 * ten
            s["p"][at, :] = I14 * s["p"][at, :] + k * (base + ten)
            s["m"][at, :] = I14 * s["m"][at, :] + k * (base - ten)
            s["t"][at, :] = I14 * s["t"][at, :] + (0.25 * k) * shear
        for i in range(chunks):
            a = 8 + 8 * i
            at, up, down = slice(a, a + 8), slice(a + 1, a + 9), slice(a - 1, a + 7)
            here = slice(8 * i, 8 * i + 8)
            p, t = s["p"][at, :], s["t"][at, :]
            fx = 0.25 * ((roll(p, -1) - roll(p, 1)) + (s["t"][up, :] - s["t"][down, :]))
            fy = 0.25 * ((roll(t, -1) - roll(t, 1)) + (s["m"][up, :] - s["m"][down, :]))
            u, v = s["u"][at, :], s["v"][at, :]
            ou, ov = s["ou"][here, :], s["ov"][here, :]
            du, dv = ou - u, ov - v
            g = du * du + dv * dv + 0.01
            drag = g * lax.rsqrt(g)
            inertia, turn = s["inertia"][here, :], s["turn"][here, :]
            diag = inertia + drag
            rx = inertia * u + fx + s["wx"][here, :] + drag * ou
            ry = inertia * v + fy + s["wy"][here, :] + drag * ov
            w = s["cover"][here, :] / (diag * diag + turn * turn)
            s["u"][at, :] = w * (diag * rx + turn * ry)
            s["v"][at, :] = w * (diag * ry - turn * rx)
        return carry

    lax.fori_loop(0, SUBS, subcycle, 0)


def state_scratch(chunks):
    tall = pltpu.VMEM((8 * chunks + 16, LANES), F32)
    flat = pltpu.VMEM((8 * chunks, LANES), F32)
    return [tall] * len(STATE) + [flat] * len(STATIC)


def named(scratch):
    return dict(zip(STATE + STATIC, scratch))


def at_row(i):
    return lax.axis_index("gy") * ROWS + 8 * i + lax.broadcasted_iota(jnp.int32, (8, LANES), 0)


def chunk_of(tile_ref, i):
    return [tile_ref[i * 64 + f * 8 : i * 64 + f * 8 + 8, :] for f in range(FIELDS)]


def stresses(p, m, t):
    return 0.5 * (p + m), 0.5 * (p - m), 0.5 * t


def finals(s, i):
    at = slice(8 + 8 * i, 16 + 8 * i)
    return [s["u"][at, :], s["v"][at, :], *stresses(s["p"][at, :], s["m"][at, :], s["t"][at, :])]


def inner_kernel(tile_ref, ou_ref, ov_ref, wx_ref, wy_ref, out_ref, *scratch):
    s = named(scratch)
    grid_rows = ROWS * lax.axis_size("gy")
    clear_ends(s, BANDS)
    for i in range(BANDS):
        put_ice(s, i, chunk_of(tile_ref, i), at_row(i), grid_rows)
        put_ocean(s, i, [ref[8 * i : 8 * i + 8, :] for ref in (ou_ref, ov_ref, wx_ref, wy_ref)])
    run_subcycles(s, BANDS)
    for i in range(BANDS):
        for f, x in enumerate(finals(s, i)):
            out_ref[f, 8 * i : 8 * i + 8, :] = x


def inner(tile, ocean):
    return pl.pallas_call(
        inner_kernel,
        out_shape=jax.ShapeDtypeStruct((FINAL, ROWS, LANES), F32),
        scratch_shapes=state_scratch(BANDS),
        compiler_params=pltpu.CompilerParams(vmem_limit_bytes=VMEM_BYTES),
        cost_estimate=pl.CostEstimate(flops=4_000_000, bytes_accessed=4_000_000, transcendentals=800_000),
        name="inner",
    )(tile, *ocean)


def strip(own, west, east, lane):
    x = jnp.where(lane < 64, roll(own, HALO), roll(own, -HALO))
    x = jnp.where(lane < HALO, west, x)
    return jnp.where(lane >= LANES - HALO, east, x)


def ice_strips(own, west, east, edge, lane):
    west = jnp.where(edge[0], 0.0, west)
    east = jnp.where(edge[1], 0.0, east)
    return [
        strip(own[f], roll(west, -f * HALO), roll(east, LANES - HALO - f * HALO), lane) for f in range(FIELDS)
    ]


def ocean_strips(own, sides, lane):
    return [
        strip(own[f], roll(sides, -64 - f * HALO), roll(sides, LANES - HALO - f * HALO), lane) for f in range(4)
    ]


def edges_x():
    a = lax.axis_index("gx")
    return a == 0, a == lax.axis_size("gx") - 1


def edges_y():
    b = lax.axis_index("gy")
    return b == 0, b == lax.axis_size("gy") - 1


def join(mid, strips, lane):
    x = jnp.where(lane < HALO, roll(strips, -HALO), mid)
    return jnp.where(lane >= LANES - HALO, roll(strips, HALO), x)


def send_band(band, five, pos_ref, packed_ref, stage):
    for f, x in enumerate(five):
        for h in range(2):
            at = h * FINAL * 4 + f * 4
            stage[at : at + 4, :] = x[4 * h : 4 * h + 4, :]
    rows = [stage[pl.ds(r, 2 * FINAL, stride=4), :] for r in range(4)]
    for c, x in enumerate(swap_chunks(rows)):
        pos = pos_ref[0, band * 4 + c]

        @pl.when(pos >= 0)
        def _():
            packed_ref[pl.ds(pos * 2 * FINAL, 2 * FINAL), :] = x


def drag_rows(five, ou, ov, cover):
    du, dv = five[0] - ou, five[1] - ov
    g = du * du + dv * dv + 0.01
    drag = cover * (g * lax.rsqrt(g))
    return drag * du, drag * dv


def sides_kernel(
    pos_ref, tile_ref, west_ref, east_ref, sides_ref, ou_ref, ov_ref, wx_ref, wy_ref, mid_ref,
    packed_ref, drag_ref, stage, *scratch,
):
    s = named(scratch)
    lane = lane_ids()
    grid_rows = ROWS * lax.axis_size("gy")
    edge = edges_x()
    clear_ends(s, BANDS)
    for i in range(BANDS):
        rows = slice(8 * i, 8 * i + 8)
        ice = ice_strips(chunk_of(tile_ref, i), west_ref[rows, :], east_ref[rows, :], edge, lane)
        put_ice(s, i, ice, at_row(i), grid_rows)
        own = [ref[rows, :] for ref in (ou_ref, ov_ref, wx_ref, wy_ref)]
        put_ocean(s, i, ocean_strips(own, sides_ref[rows, :], lane))
    run_subcycles(s, BANDS)
    for i in range(2, BANDS - 2):
        rows = slice(8 * i, 8 * i + 8)
        five = [join(mid_ref[f, rows, :], x, lane) for f, x in enumerate(finals(s, i))]
        send_band(i, five, pos_ref, packed_ref, stage)
        cover = tile_ref[i * 64 + 56 : i * 64 + 64, :]
        drag_ref[0, rows, :], drag_ref[1, rows, :] = drag_rows(five, ou_ref[rows, :], ov_ref[rows, :], cover)


def specs(count):
    return [pl.BlockSpec(memory_space=pltpu.SMEM)] + [pl.BlockSpec(memory_space=pltpu.VMEM)] * (count - 1)


STAGE = pltpu.VMEM((2 * FINAL * 4, LANES), F32)
RESULTS = (
    jax.ShapeDtypeStruct((2 * TILES * 2 * FINAL, LANES), F32),
    jax.ShapeDtypeStruct((2, ROWS, LANES), F32),
)


def sides(pos, tile, west, east, ocean_sides, ocean, mid):
    return pl.pallas_call(
        sides_kernel,
        in_specs=specs(10),
        out_shape=RESULTS,
        scratch_shapes=[STAGE] + state_scratch(BANDS),
        compiler_params=pltpu.CompilerParams(vmem_limit_bytes=VMEM_BYTES),
        cost_estimate=pl.CostEstimate(flops=5_000_000, bytes_accessed=5_000_000, transcendentals=800_000),
        name="sides",
    )(pos, tile, west, east, ocean_sides, *ocean, mid)


def ends_kernel(
    pos_ref, tile_ref, west_ref, east_ref, north_ref, south_ref, sides_ref, osea_ref, nsea_ref,
    ou_ref, ov_ref, wx_ref, wy_ref, packed_in, drag_in, packed_ref, drag_ref, stage, *scratch,
):
    packed_ref[...] = packed_in[...]
    drag_ref[...] = drag_in[...]
    s = named(scratch)
    lane = lane_ids()
    grid_rows = ROWS * lax.axis_size("gy")
    edge = edges_x()
    outside = edges_y()
    ocean_refs = (ou_ref, ov_ref, wx_ref, wy_ref)
    clear_ends(s, 24)
    for end in range(2):
        ref, sea = ((north_ref, nsea_ref), (south_ref, osea_ref))[end]
        for j in range(6):
            i = (j - 2) if end == 0 else BANDS - 4 + j
            if 0 <= i < BANDS:
                rows = slice(8 * i, 8 * i + 8)
                own = chunk_of(tile_ref, i)
                west, east, near = west_ref[rows, :], east_ref[rows, :], sides_ref[rows, :]
                water = [x[rows, :] for x in ocean_refs]
            else:
                h = i % BANDS % 2
                own = [jnp.where(outside[end], 0.0, x) for x in chunk_of(ref, h)]
                west = jnp.where(outside[end], 0.0, ref[128 + 8 * h : 136 + 8 * h, :])
                east = jnp.where(outside[end], 0.0, ref[144 + 8 * h : 152 + 8 * h, :])
                near = sea[64 + 8 * h : 72 + 8 * h, :]
                water = [sea[16 * f + 8 * h : 16 * f + 8 * h + 8, :] for f in range(4)]
            for part in range(2):
                chunk = part * 12 + end * 6 + j
                put_ice(
                    s, chunk, ice_strips(own, west, east, edge, lane) if part else own, at_row(i), grid_rows
                )
                put_ocean(s, chunk, ocean_strips(water, near, lane) if part else water)
    run_subcycles(s, 24)
    for end in range(2):
        for j in (2, 3):
            i = (j - 2) if end == 0 else BANDS - 4 + j
            rows = slice(8 * i, 8 * i + 8)
            chunk = end * 6 + j
            five = [join(x, y, lane) for x, y in zip(finals(s, chunk), finals(s, chunk + 12))]
            send_band(i, five, pos_ref, packed_ref, stage)
            cover = tile_ref[i * 64 + 56 : i * 64 + 64, :]
            drag_ref[0, rows, :], drag_ref[1, rows, :] = drag_rows(
                five, ou_ref[rows, :], ov_ref[rows, :], cover
            )


def ends(pos, tile, west, east, north, south, ocean_sides, ocean_south, ocean_north, ocean, packed, drag):
    return pl.pallas_call(
        ends_kernel,
        in_specs=specs(15),
        out_shape=RESULTS,
        scratch_shapes=[STAGE] + state_scratch(24),
        compiler_params=pltpu.CompilerParams(vmem_limit_bytes=VMEM_BYTES),
        name="ends",
    )(pos, tile, west, east, north, south, ocean_sides, ocean_south, ocean_north, *ocean, packed, drag)


def unpack_ice_kernel(starts_ref, recv_ref, vel_ref, str_ref, blk):
    for t in range(TILES):
        start = starts_ref[0, t]
        for c in range(2):
            at = (2 * t + c) * 2 * FINAL
            blk[start + c, 0 : 2 * FINAL, :] = recv_ref[at : at + 2 * FINAL, :]

    def some(g, carry):
        for j in range(8):
            i = g * 8 + j
            for h in range(2):
                cut = slice(h * LANES, (h + 1) * LANES)
                vel_ref[i, :, cut] = blk[i, h * FINAL : h * FINAL + 2, :]
                str_ref[i, :, cut] = blk[i, h * FINAL + 2 : h * FINAL + 5, :]
        return carry

    lax.fori_loop(0, SLOTS // 8, some, 0)


def unpack_ice(starts, recv):
    return pl.pallas_call(
        unpack_ice_kernel,
        in_specs=specs(2),
        out_shape=(
            jax.ShapeDtypeStruct((SLOTS, 2, 2 * LANES), F32),
            jax.ShapeDtypeStruct((SLOTS, 3, 2 * LANES), F32),
        ),
        scratch_shapes=[pltpu.VMEM((SLOTS + 8, 16, LANES), F32)],
        compiler_params=pltpu.CompilerParams(vmem_limit_bytes=VMEM_BYTES),
        name="unpack_ice",
    )(starts, recv)


def both_ways(axis, forward, backward):
    n = lax.axis_size(axis)
    return (
        lax.ppermute(forward, axis, [(i, (i + 1) % n) for i in range(n)]),
        lax.ppermute(backward, axis, [((i + 1) % n, i) for i in range(n)]),
    )


def on_device(
    owner_list, ice_mask, velocity, stress, thickness, concentration, ocean_u, ocean_v, wind_x, wind_y, surface_temp
):
    ocean = (ocean_u, ocean_v, wind_x, wind_y)
    outbound, starts, pos = pack_ice(owner_list, ice_mask, velocity, stress, thickness, concentration)
    arrived = lax.all_to_all(outbound, AXES, split_axis=0, concat_axis=0, tiled=True)

    rim = ocean_edges(*ocean)
    from_west, from_east = both_ways("gx", rim, rim)
    ocean_sides = jnp.where(lane_ids(ROWS) < 64, from_east, from_west)
    low = jnp.concatenate([x[:HALO] for x in ocean] + [ocean_sides[:HALO]], axis=0)
    high = jnp.concatenate([x[-HALO:] for x in ocean] + [ocean_sides[-HALO:]], axis=0)
    ocean_north, ocean_south = both_ways("gy", high, low)

    tile, west_edge, east_edge = unpack_tile(pos, arrived, surface_temp)
    west, east = both_ways("gx", east_edge, west_edge)
    mid = inner(tile, ocean)
    low = jnp.concatenate([tile[:128], west[:HALO], east[:HALO]], axis=0)
    high = jnp.concatenate([tile[-128:], west[-HALO:], east[-HALO:]], axis=0)
    north, south = both_ways("gy", high, low)
    packed, drag = sides(pos, tile, west, east, ocean_sides, ocean, mid)
    packed, drag = ends(
        pos, tile, west, east, north, south, ocean_sides, ocean_south, ocean_north, ocean, packed, drag
    )

    homeward = packed.reshape(2 * TILES, FINAL, 2, LANES)
    back = lax.all_to_all(homeward, AXES, split_axis=0, concat_axis=0, tiled=True)
    vel, strs = unpack_ice(starts, back.reshape(2 * TILES * 2 * FINAL, LANES))
    return vel, strs, drag


def solution(mesh):
    blocks = P(AXES, None, None)
    return jax.shard_map(
        on_device,
        mesh=mesh,
        in_specs=(P(), P(AXES, None)) + (blocks,) * 4 + (P("gy", "gx"),) * 5,
        out_specs=(blocks, blocks, P(None, "gy", "gx")),
        check_vma=False,
    )
```

```python
import jax
import jax.numpy as jnp
from jax import lax
from jax.experimental import pallas as pl
from jax.experimental.pallas import tpu as pltpu
from jax.sharding import PartitionSpec as P

AXES = ("gx", "gy")
TILES = 128
SLOTS = 112
ROWS = 256
LANES = 128
BANDS = ROWS // 8
HALO = 16
SUBS = 8
FIELDS = 8
FINAL = 5
I14 = 1.0 / 1.4
F32 = jnp.float32
VMEM_BYTES = 24 * 1024 * 1024


def specs(count):
    return [pl.BlockSpec(memory_space=pltpu.SMEM)] + [pl.BlockSpec(memory_space=pltpu.VMEM)] * (count - 1)


def lane_ids(rows=8):
    return lax.broadcasted_iota(jnp.int32, (rows, LANES), 1)


def roll(x, shift):
    return pltpu.roll(x, shift % LANES, 1)


def interleave(tasks, width):
    tasks = list(tasks)
    active = []
    while tasks or active:
        if tasks and len(active) < width:
            active.append(tasks.pop(0))
        running = []
        for task in active:
            try:
                next(task)
                running.append(task)
            except StopIteration:
                pass
        active = running


def swap_chunks(quads):
    lane = lane_ids(quads[0][0].shape[0])
    low, even = lane < 64, (lane & 32) == 0
    far = [(roll(jnp.where(low, c, a), 64), roll(jnp.where(low, d, b), 64)) for a, b, c, d in quads]
    yield
    quads = [
        (jnp.where(low, a, ac), jnp.where(low, b, bd), jnp.where(low, ac, c), jnp.where(low, bd, d))
        for (a, b, c, d), (ac, bd) in zip(quads, far)
    ]
    near = [(roll(b, 32), roll(a, 96), roll(d, 32), roll(c, 96)) for a, b, c, d in quads]
    yield
    return [
        (jnp.where(even, a, p), jnp.where(even, q, b), jnp.where(even, c, r), jnp.where(even, t, d))
        for (a, b, c, d), (p, q, r, t) in zip(quads, near)
    ]


def pack_kernel(*refs):
    far, refs = refs[:11], refs[11:]
    (out_ref, starts_ref, pos_ref, west_ref, east_ref), refs = refs[:5], refs[5:]
    here, (blk, near, sem, sems) = refs[:11], refs[11:]
    ou_ref, ov_ref, wx_ref, wy_ref, _, owner_ref, con_ref, thk_ref, str_ref, mask_ref, vel_ref = here
    loads = [pltpu.make_async_copy(x, y, sems.at[n]) for n, (x, y) in enumerate(zip(far, here))]
    for n in (*range(5, 11), *range(5)):
        loads[n].start()
    loads[5].wait()
    me = lax.axis_index("gx") * lax.axis_size("gy") + lax.axis_index("gy")
    first = lax.broadcasted_iota(jnp.int32, (TILES, TILES), 0)
    second = lax.broadcasted_iota(jnp.int32, (TILES, TILES), 1)
    before = jnp.where(first < second, 1.0, 0.0)
    ones = jnp.ones((8, TILES), F32)
    owned = jnp.where(owner_ref[...] == me, 1.0, 0.0)
    counts = lax.dot_general(ones, owned, (((1,), (1,)), ((), ())), preferred_element_type=F32)
    starts = jnp.dot(counts, before, preferred_element_type=F32)
    starts_ref[...] = starts.astype(jnp.int32)
    copy = pltpu.make_async_copy(starts_ref, near, sem)
    copy.start()

    mine = jnp.broadcast_to(owner_ref[pl.ds(me, 1), :], (TILES, TILES)).astype(F32)
    column = mine.T
    rank = jnp.dot(ones, jnp.where(column == mine, before, 0.0), preferred_element_type=F32)
    per_owner = jnp.dot(ones, jnp.where(column == second.astype(F32), 1.0, 0.0), preferred_element_type=F32)
    lane = lane_ids().astype(F32)
    free = jnp.min(jnp.where(per_owner < 2.0, lane, 1000.0), axis=1, keepdims=True)
    mine = mine[:8]
    icy = mine < TILES
    slot = jnp.where(icy, 2.0 * mine + rank, 2.0 * free + 1.0)
    row = lax.broadcasted_iota(jnp.int32, (8, TILES), 0)
    pos_ref[...] = jnp.where(row == 0, slot, jnp.where(icy, 1.0, 0.0)).astype(jnp.int32)

    for n in range(6, 11):
        loads[n].wait()
    for g in range(SLOTS // 8):
        eight = slice(8 * g, 8 * g + 8)
        for h in range(2):
            cut = slice(h * LANES, (h + 1) * LANES)
            con = [con_ref[c, eight, cut] for c in range(5)]
            mass = sum(thk_ref[c, eight, cut] * con[c] for c in range(5))
            strength = mass * jnp.exp(-20.0 * (1.0 - sum(con)))
            rows = [str_ref[f, eight, cut] for f in range(3)]
            rows += [strength, mass, mask_ref[eight, cut].astype(F32)]
            for f, x in enumerate(rows):
                blk[pl.ds(128 * g + 8 * h + 2 + f, 8, stride=16), :] = x
            for j in range(8):
                at = 128 * g + 16 * j + 8 * h
                blk[at : at + 2, :] = vel_ref[8 * g + j, :, cut]

    for n in range(5):
        loads[n].wait()
    chunk = lane_ids() // HALO

    def sea_edges(i):
        moved = []
        for half in range(2):
            rows = slice(8 * i + half * LANES, 8 * i + half * LANES + 8)
            for f, ref in enumerate((ou_ref, ov_ref, wx_ref, wy_ref)):
                moved.append(roll(ref[rows, :], (4 * half + f) * HALO))
        yield
        west, east = moved[0], moved[0]
        for n in range(1, 8):
            west = jnp.where(chunk == n, moved[n], west)
            east = jnp.where(chunk == n - 1, moved[n], east)
        west_ref[8 * i : 8 * i + 8, :] = west
        east_ref[8 * i : 8 * i + 8, :] = east

    interleave([sea_edges(i) for i in range(BANDS // 2)], 5)

    copy.wait()
    for t in range(TILES):
        at = pl.multiple_of(near[0, t] * 16, 16)
        out_ref[2 * t] = blk[pl.ds(at, 16), :]
        out_ref[2 * t + 1] = blk[pl.ds(at + 16, 16), :]


def pack(owner_list, ice_mask, velocity, stress, thickness, concentration, maps):
    def by_field(x):
        return jnp.transpose(x, (1, 0, 2))

    inputs = (
        *maps, owner_list, by_field(concentration), by_field(thickness), by_field(stress), ice_mask, velocity
    )
    return pl.pallas_call(
        pack_kernel,
        in_specs=[pl.BlockSpec(memory_space=pltpu.HBM)] * 11,
        out_shape=(
            jax.ShapeDtypeStruct((2 * TILES, 2 * FIELDS, LANES), F32),
            jax.ShapeDtypeStruct((8, TILES), jnp.int32),
            jax.ShapeDtypeStruct((8, TILES), jnp.int32),
            jax.ShapeDtypeStruct((ROWS // 2, LANES), F32),
            jax.ShapeDtypeStruct((ROWS // 2, LANES), F32),
        )
        + (jax.ShapeDtypeStruct((ROWS, LANES), F32),) * 5,
        scratch_shapes=[pltpu.VMEM(x.shape, x.dtype) for x in inputs[5:]]
        + [
            pltpu.VMEM(((SLOTS + 8) * 16, LANES), F32),
            pltpu.SMEM((8, TILES), jnp.int32),
            pltpu.SemaphoreType.DMA(()),
            pltpu.SemaphoreType.DMA((11,)),
        ],
        compiler_params=pltpu.CompilerParams(vmem_limit_bytes=VMEM_BYTES),
        name="pack",
    )(*(pltpu.with_memory_space_constraint(x, pltpu.HBM) for x in inputs))


def unpack_tile_kernel(pos_ref, recv_ref, temp_ref, sea_west_ref, sea_east_ref, tile_ref, west_ref, east_ref):
    chunk = lane_ids() // HALO

    def band(i):
        base = i * 64
        rows = slice(8 * i, 8 * i + 8)
        quads = []
        for h in range(2):
            four = []
            for k in range(4 * i, 4 * i + 4):
                got = recv_ref[pos_ref[0, k], h * FIELDS : (h + 1) * FIELDS, :]
                four.append(jnp.where(pos_ref[1, k] > 0, got, 0.0))
            quads.append(four)
        quads = yield from swap_chunks(quads)
        for h in range(2):
            for r, x in enumerate(quads[h]):
                tile_ref[pl.ds(base + h * 4 + r, FIELDS, stride=8), :] = x
        melt = jnp.exp(-0.5 * jnp.maximum(temp_ref[rows, :], 0.0))
        yield
        moved = []
        for f in range(FIELDS):
            at = slice(base + 8 * f, base + 8 * f + 8)
            x = tile_ref[at, :]
            if f == 5:
                x = x * melt
                tile_ref[at, :] = x
            moved.append(roll(x, f * HALO))
        yield
        west, east = moved[0], moved[0]
        for f in range(1, FIELDS):
            west = jnp.where(chunk == f, moved[f], west)
            east = jnp.where(chunk == f - 1, moved[f], east)
        west_ref[rows, :] = west
        east_ref[rows, :] = east

    interleave([band(i) for i in range(BANDS)], 5)
    west_ref[ROWS:, :] = sea_west_ref[...]
    east_ref[ROWS:, :] = sea_east_ref[...]


EDGE = ROWS + ROWS // 2


def unpack_tile(pos, recv, temp, sea_west, sea_east):
    return pl.pallas_call(
        unpack_tile_kernel,
        in_specs=specs(5),
        out_shape=(
            jax.ShapeDtypeStruct((BANDS * FIELDS * 8, LANES), F32),
            jax.ShapeDtypeStruct((EDGE, LANES), F32),
            jax.ShapeDtypeStruct((EDGE, LANES), F32),
        ),
        compiler_params=pltpu.CompilerParams(vmem_limit_bytes=VMEM_BYTES),
        name="unpack_tile",
    )(pos, recv, temp, sea_west, sea_east)


STATE = ("u", "v", "p", "m", "t")
STATIC = ("ou", "ov", "wx", "wy", "inertia", "turn", "k", "cover")


def put_ice(s, i, ice, row_ids, grid_rows):
    u, v, total, diff, shear, strength, mass, cover = ice
    at = slice(8 + 8 * i, 16 + 8 * i)
    here = slice(8 * i, 8 * i + 8)
    s["u"][at, :] = u
    s["v"][at, :] = v
    s["p"][at, :] = cover * (total + diff)
    s["m"][at, :] = cover * (total - diff)
    s["t"][at, :] = cover * (shear + shear)
    coriolis = 2.0 * (row_ids.astype(F32) + 0.5) / grid_rows - 1.0
    s["inertia"][here, :] = 2.0 * mass
    s["turn"][here, :] = mass * coriolis
    s["k"][here, :] = (0.4 * I14) * (cover * strength)
    s["cover"][here, :] = cover


def put_ocean(s, i, ocean):
    here = slice(8 * i, 8 * i + 8)
    for name, x in zip(("ou", "ov", "wx", "wy"), ocean):
        s[name][here, :] = x


def clear_ends(s, chunks):
    zero = jnp.zeros((8, LANES), F32)
    for name in STATE:
        s[name][0:8, :] = zero
        s[name][8 + 8 * chunks : 16 + 8 * chunks, :] = zero


def run_subcycles(s, chunks, times):
    def subcycle(step, carry):
        for i in chunks:
            a = 8 + 8 * i
            at, up, down = slice(a, a + 8), slice(a + 1, a + 9), slice(a - 1, a + 7)
            here = slice(8 * i, 8 * i + 8)
            u, v = s["u"][at, :], s["v"][at, :]
            exx = roll(u, -1) - roll(u, 1)
            eyy = s["v"][up, :] - s["v"][down, :]
            shear = (s["u"][up, :] - s["u"][down, :]) + (roll(v, -1) - roll(v, 1))
            div = exx + eyy
            ten = exx - eyy
            q = div * div + 0.25 * (ten * ten + shear * shear) + 0.04
            inv = lax.rsqrt(q)
            k = s["k"][here, :] * inv
            base = div - q * inv
            ten = 0.25 * ten
            s["p"][at, :] = I14 * s["p"][at, :] + k * (base + ten)
            s["m"][at, :] = I14 * s["m"][at, :] + k * (base - ten)
            s["t"][at, :] = I14 * s["t"][at, :] + (0.25 * k) * shear
        for i in chunks:
            a = 8 + 8 * i
            at, up, down = slice(a, a + 8), slice(a + 1, a + 9), slice(a - 1, a + 7)
            here = slice(8 * i, 8 * i + 8)
            p, t = s["p"][at, :], s["t"][at, :]
            fx = 0.25 * ((roll(p, -1) - roll(p, 1)) + (s["t"][up, :] - s["t"][down, :]))
            fy = 0.25 * ((roll(t, -1) - roll(t, 1)) + (s["m"][up, :] - s["m"][down, :]))
            u, v = s["u"][at, :], s["v"][at, :]
            ou, ov = s["ou"][here, :], s["ov"][here, :]
            du, dv = ou - u, ov - v
            g = du * du + dv * dv + 0.01
            drag = g * lax.rsqrt(g)
            inertia, turn = s["inertia"][here, :], s["turn"][here, :]
            diag = inertia + drag
            rx = inertia * u + fx + s["wx"][here, :] + drag * ou
            ry = inertia * v + fy + s["wy"][here, :] + drag * ov
            w = s["cover"][here, :] / (diag * diag + turn * turn)
            s["u"][at, :] = w * (diag * rx + turn * ry)
            s["v"][at, :] = w * (diag * ry - turn * rx)
        return carry

    lax.fori_loop(0, times, subcycle, 0)


def state_scratch(chunks):
    tall = pltpu.VMEM((8 * chunks + 16, LANES), F32)
    flat = pltpu.VMEM((8 * chunks, LANES), F32)
    return [tall] * len(STATE) + [flat] * len(STATIC)


def named(scratch):
    return dict(zip(STATE + STATIC, scratch))


def at_row(i):
    return lax.axis_index("gy") * ROWS + 8 * i + lax.broadcasted_iota(jnp.int32, (8, LANES), 0)


def chunk_of(tile_ref, i):
    return [tile_ref[i * 64 + f * 8 : i * 64 + f * 8 + 8, :] for f in range(FIELDS)]


def stresses(p, m, t):
    return 0.5 * (p + m), 0.5 * (p - m), 0.5 * t


def finals(s, i):
    at = slice(8 + 8 * i, 16 + 8 * i)
    return [s["u"][at, :], s["v"][at, :], *stresses(s["p"][at, :], s["m"][at, :], s["t"][at, :])]


def inner_kernel(tile_ref, ou_ref, ov_ref, wx_ref, wy_ref, out_ref, *scratch):
    s = named(scratch)
    grid_rows = ROWS * lax.axis_size("gy")
    clear_ends(s, BANDS)
    for i in range(BANDS):
        put_ice(s, i, chunk_of(tile_ref, i), at_row(i), grid_rows)
        put_ocean(s, i, [ref[8 * i : 8 * i + 8, :] for ref in (ou_ref, ov_ref, wx_ref, wy_ref)])
    run_subcycles(s, range(BANDS), SUBS)
    for i in range(BANDS):
        for f, x in enumerate(finals(s, i)):
            out_ref[f, 8 * i : 8 * i + 8, :] = x


def inner(tile, ocean):
    return pl.pallas_call(
        inner_kernel,
        out_shape=jax.ShapeDtypeStruct((FINAL, ROWS, LANES), F32),
        scratch_shapes=state_scratch(BANDS),
        compiler_params=pltpu.CompilerParams(vmem_limit_bytes=VMEM_BYTES),
        cost_estimate=pl.CostEstimate(flops=4_000_000, bytes_accessed=4_000_000, transcendentals=800_000),
        name="inner",
    )(tile, *ocean)


def strip_moves(own, west, east, chunk):
    return own, roll(own, -32), roll(west, (8 - chunk) * HALO), roll(east, (6 - chunk) * HALO)


def strip(own, moved, west, east, lane):
    x = jnp.where(lane < 48, own, moved)
    x = jnp.where(lane >= 112, west, x)
    return jnp.where((lane >= 96) & (lane < 112), east, x)


def ice_strips(own, west, east, edge, lane):
    west = jnp.where(edge[0], 0.0, west)
    east = jnp.where(edge[1], 0.0, east)
    moved = [strip_moves(own[f], west, east, f) for f in range(FIELDS)]
    yield
    return [strip(*x, lane) for x in moved]


def ocean_strips(own, west, east, half, lane):
    moved = [strip_moves(own[f], west, east, 4 * half + f) for f in range(4)]
    yield
    return [strip(*x, lane) for x in moved]


def edges_x():
    a = lax.axis_index("gx")
    return a == 0, a == lax.axis_size("gx") - 1


def edges_y():
    b = lax.axis_index("gy")
    return b == 0, b == lax.axis_size("gy") - 1


def join(mid, strips, moved, lane):
    x = jnp.where(lane < HALO, strips, mid)
    return jnp.where(lane >= LANES - HALO, moved, x)


def finish_band(band, mids, strips, refs, stage, lane):
    pos_ref, tile_ref, ou_ref, ov_ref, packed_ref, drag_ref = refs
    moved = [roll(x, 32) for x in strips]
    yield
    five = [join(*x, lane) for x in zip(mids, strips, moved)]
    for f, x in enumerate(five):
        for h in range(2):
            at = h * FINAL * 4 + f * 4
            stage[at : at + 4, :] = x[4 * h : 4 * h + 4, :]
    rows = slice(8 * band, 8 * band + 8)
    cover = tile_ref[band * 64 + 56 : band * 64 + 64, :]
    drag_ref[0, rows, :], drag_ref[1, rows, :] = drag_rows(five, ou_ref[rows, :], ov_ref[rows, :], cover)
    yield
    quad = [stage[pl.ds(r, 2 * FINAL, stride=4), :] for r in range(4)]
    (quad,) = yield from swap_chunks([quad])
    for c, x in enumerate(quad):
        packed_ref[pl.ds(pos_ref[0, band * 4 + c] * 2 * FINAL, 2 * FINAL), :] = x


def drag_rows(five, ou, ov, cover):
    du, dv = five[0] - ou, five[1] - ov
    g = du * du + dv * dv + 0.01
    drag = cover * (g * lax.rsqrt(g))
    return drag * du, drag * dv


def sides_kernel(
    pos_ref, tile_ref, west_ref, east_ref, ou_ref, ov_ref, wx_ref, wy_ref, mid_ref, packed_ref, drag_ref, stage, *scratch,
):
    s = named(scratch)
    lane = lane_ids()
    grid_rows = ROWS * lax.axis_size("gy")
    edge = edges_x()
    clear_ends(s, BANDS)

    def start(i):
        rows = slice(8 * i, 8 * i + 8)
        ice = yield from ice_strips(chunk_of(tile_ref, i), west_ref[rows, :], east_ref[rows, :], edge, lane)
        put_ice(s, i, ice, at_row(i), grid_rows)
        half, j = divmod(i, BANDS // 2)
        sea = slice(ROWS + 8 * j, ROWS + 8 * j + 8)
        own = [ref[rows, :] for ref in (ou_ref, ov_ref, wx_ref, wy_ref)]
        put_ocean(s, i, (yield from ocean_strips(own, west_ref[sea, :], east_ref[sea, :], half, lane)))

    interleave([start(i) for i in range(BANDS)], 3)
    run_subcycles(s, range(BANDS), SUBS)
    refs = (pos_ref, tile_ref, ou_ref, ov_ref, packed_ref, drag_ref)

    def finish(i):
        mids = [mid_ref[f, 8 * i : 8 * i + 8, :] for f in range(FINAL)]
        yield from finish_band(i, mids, finals(s, i), refs, stage.at[i], lane)

    interleave([finish(i) for i in range(2, BANDS - 2)], 6)


def stage_scratch(bands):
    return [pltpu.VMEM((bands, 2 * FINAL * 4, LANES), F32)]


RESULTS = (
    jax.ShapeDtypeStruct((2 * TILES * 2 * FINAL, LANES), F32),
    jax.ShapeDtypeStruct((2, ROWS, LANES), F32),
)


def sides(pos, tile, west, east, ocean, mid):
    return pl.pallas_call(
        sides_kernel,
        in_specs=specs(9),
        out_shape=RESULTS,
        scratch_shapes=stage_scratch(BANDS) + state_scratch(BANDS),
        compiler_params=pltpu.CompilerParams(vmem_limit_bytes=VMEM_BYTES),
        cost_estimate=pl.CostEstimate(flops=5_000_000, bytes_accessed=5_000_000, transcendentals=800_000),
        name="sides",
    )(pos, tile, west, east, *ocean, mid)


def ends_kernel(
    pos_ref, tile_ref, west_ref, east_ref, north_ref, south_ref, ou_ref, ov_ref, wx_ref, wy_ref,
    packed_in, drag_in, packed_ref, drag_ref, stage, *scratch,
):
    packed_ref[...] = packed_in[...]
    drag_ref[...] = drag_in[...]
    s = named(scratch)
    lane = lane_ids()
    grid_rows = ROWS * lax.axis_size("gy")
    edge = edges_x()
    outside = edges_y()
    ocean_refs = (ou_ref, ov_ref, wx_ref, wy_ref)
    clear_ends(s, 24)

    def start(end, j):
        ref = (north_ref, south_ref)[end]
        i = (j - 2) if end == 0 else BANDS - 4 + j
        half = 1 - end if not 0 <= i < BANDS else i // (BANDS // 2)
        if 0 <= i < BANDS:
            rows = slice(8 * i, 8 * i + 8)
            own = chunk_of(tile_ref, i)
            west, east = west_ref[rows, :], east_ref[rows, :]
            water = [x[rows, :] for x in ocean_refs]
            at = ROWS + 8 * (i % (BANDS // 2))
            sea_west, sea_east = west_ref[at : at + 8, :], east_ref[at : at + 8, :]
        else:
            at = 8 * (i % 2)

            def part_of(base):
                return ref[base + at : base + at + 8, :]

            own = [jnp.where(outside[end], 0.0, x) for x in chunk_of(ref, i % 2)]
            west = jnp.where(outside[end], 0.0, part_of(128))
            east = jnp.where(outside[end], 0.0, part_of(144))
            water = [part_of(160 + 16 * f) for f in range(4)]
            sea_west, sea_east = part_of(224), part_of(240)
        for part in range(2):
            chunk = part * 12 + end * 6 + j
            ice = (yield from ice_strips(own, west, east, edge, lane)) if part else own
            put_ice(s, chunk, ice, at_row(i), grid_rows)
            if part:
                water = yield from ocean_strips(water, sea_west, sea_east, half, lane)
            put_ocean(s, chunk, water)

    interleave([start(end, j) for end in range(2) for j in range(6)], 3)
    run_subcycles(s, range(24), SUBS // 2)
    run_subcycles(s, [c for c in range(24) if c % 6 not in (0, 5)], SUBS // 2)
    refs = (pos_ref, tile_ref, ou_ref, ov_ref, packed_ref, drag_ref)

    def finish(n):
        end, j = divmod(n, 2)
        chunk = end * 6 + j + 2
        i = BANDS - 2 + j if end else j
        yield from finish_band(i, finals(s, chunk), finals(s, chunk + 12), refs, stage.at[n], lane)

    interleave([finish(n) for n in range(4)], 4)


def ends(pos, tile, west, east, north, south, ocean, packed, drag):
    return pl.pallas_call(
        ends_kernel,
        in_specs=specs(12),
        out_shape=RESULTS,
        scratch_shapes=stage_scratch(4) + state_scratch(24),
        compiler_params=pltpu.CompilerParams(vmem_limit_bytes=VMEM_BYTES),
        name="ends",
    )(pos, tile, west, east, north, south, *ocean, packed, drag)


def unpack_ice_kernel(starts_ref, recv_ref, vel_ref, str_ref, blk):
    for t in range(TILES):
        start = starts_ref[0, t]
        for c in range(2):
            at = (2 * t + c) * 2 * FINAL
            to = pl.multiple_of((start + c) * 16, 16)
            blk[pl.ds(to, 2 * FINAL), :] = recv_ref[at : at + 2 * FINAL, :]
    for g in range(SLOTS // 8):
        eight = slice(8 * g, 8 * g + 8)
        for h in range(2):
            cut = slice(h * LANES, (h + 1) * LANES)
            for f in range(3):
                str_ref[f, eight, cut] = blk[pl.ds(128 * g + h * FINAL + 2 + f, 8, stride=16), :]
            for j in range(8):
                at = 128 * g + 16 * j + h * FINAL
                vel_ref[8 * g + j, :, cut] = blk[at : at + 2, :]


def unpack_ice(starts, recv):
    vel, strs = pl.pallas_call(
        unpack_ice_kernel,
        in_specs=specs(2),
        out_shape=(
            jax.ShapeDtypeStruct((SLOTS, 2, 2 * LANES), F32),
            jax.ShapeDtypeStruct((3, SLOTS, 2 * LANES), F32),
        ),
        scratch_shapes=[pltpu.VMEM(((SLOTS + 8) * 16, LANES), F32)],
        compiler_params=pltpu.CompilerParams(vmem_limit_bytes=VMEM_BYTES),
        name="unpack_ice",
    )(starts, recv)
    return vel, jnp.transpose(strs, (1, 0, 2))


def both_ways(axis, forward, backward):
    n = lax.axis_size(axis)
    return (
        lax.ppermute(forward, axis, [(i, (i + 1) % n) for i in range(n)]),
        lax.ppermute(backward, axis, [((i + 1) % n, i) for i in range(n)]),
    )


def on_device(
    owner_list, ice_mask, velocity, stress, thickness, concentration, ocean_u, ocean_v, wind_x, wind_y, surface_temp
):
    ocean = (ocean_u, ocean_v, wind_x, wind_y)
    outbound, starts, pos, sea_west, sea_east, *maps = pack(
        owner_list, ice_mask, velocity, stress, thickness, concentration, (*ocean, surface_temp)
    )
    *ocean, surface_temp = maps
    arrived = lax.all_to_all(outbound, AXES, split_axis=0, concat_axis=0, tiled=True)
    tile, west_edge, east_edge = unpack_tile(pos, arrived, surface_temp, sea_west, sea_east)
    west, east = both_ways("gx", east_edge, west_edge)
    west, east, mid = lax.optimization_barrier((west, east, inner(tile, ocean)))

    def edge(cells, block_rows, sea_rows):
        parts = [tile[block_rows], west[:ROWS][cells], east[:ROWS][cells]]
        parts += [x[cells] for x in ocean] + [west[sea_rows], east[sea_rows]]
        return jnp.concatenate(parts, axis=0)

    low = edge(slice(0, HALO), slice(0, 128), slice(ROWS, ROWS + HALO))
    high = edge(slice(ROWS - HALO, ROWS), slice(-128, None), slice(EDGE - HALO, EDGE))
    north, south = both_ways("gy", high, low)
    packed, drag = sides(pos, tile, west, east, ocean, mid)
    packed, drag = ends(pos, tile, west, east, north, south, ocean, packed, drag)

    homeward = packed.reshape(2 * TILES, FINAL, 2, LANES)
    back = lax.all_to_all(homeward, AXES, split_axis=0, concat_axis=0, tiled=True)
    vel, strs = unpack_ice(starts, back.reshape(2 * TILES * 2 * FINAL, LANES))
    return vel, strs, drag


def solution(mesh):
    blocks = P(AXES, None, None)
    return jax.shard_map(
        on_device,
        mesh=mesh,
        in_specs=(P(), P(AXES, None)) + (blocks,) * 4 + (P("gy", "gx"),) * 5,
        out_specs=(blocks, blocks, P(None, "gy", "gx")),
        check_vma=False,
    )
```

```python
import jax
import jax.numpy as jnp
from jax import lax
from jax.experimental import pallas as pl
from jax.experimental.pallas import tpu as pltpu
from jax.sharding import PartitionSpec as P

AXES = ("gx", "gy")
TILES = 128
SLOTS = 112
ROWS = 256
LANES = 128
BANDS = ROWS // 8
HALO = 16
SUBS = 8
FIELDS = 8
FINAL = 5
I14 = 1.0 / 1.4
F32 = jnp.float32
VMEM_BYTES = 24 * 1024 * 1024


def specs(count):
    return [pl.BlockSpec(memory_space=pltpu.SMEM)] + [pl.BlockSpec(memory_space=pltpu.VMEM)] * (count - 1)


def lane_ids(rows=8):
    return lax.broadcasted_iota(jnp.int32, (rows, LANES), 1)


def roll(x, shift):
    return pltpu.roll(x, shift % LANES, 1) if shift % LANES else x


def interleave(tasks, width):
    tasks = list(tasks)
    active = []
    while tasks or active:
        if tasks and len(active) < width:
            active.append(tasks.pop(0))
        running = []
        for task in active:
            try:
                next(task)
                running.append(task)
            except StopIteration:
                pass
        active = running


def swap_chunks(quads, room):
    chunk = lane_ids() // 32
    moved = [[roll(x, 32 * c) for c, x in enumerate(quad)] for quad in quads]
    yield
    for q, quad in enumerate(moved):
        for c, x in enumerate(quad):
            room[q, c] = x
    yield
    out = []
    for q in range(len(quads)):
        kept = [room[q, c] for c in range(4)]
        rows = []
        for r in range(4):
            x = kept[-r % 4]
            for to in range(1, 4):
                x = jnp.where(chunk == to, kept[(to - r) % 4], x)
            rows.append(roll(x, -32 * r))
        out.append(rows)
    yield
    return out


def pack_kernel(*refs):
    far, refs = refs[:11], refs[11:]
    (out_ref, starts_ref, pos_ref, west_ref, east_ref), refs = refs[:5], refs[5:]
    here, (blk, starts_v, pos_v, scalars, sems) = refs[:11], refs[11:]
    ou_ref, ov_ref, wx_ref, wy_ref, _, owner_ref, con_ref, thk_ref, str_ref, mask_ref, vel_ref = here
    loads = [pltpu.make_async_copy(x, y, sems.at[n]) for n, (x, y) in enumerate(zip(far, here))]
    for n in (5, 0, 1, 2, 3, 6, 7, 8, 9, 10, 4):
        loads[n].start()
    loads[5].wait()
    me = lax.axis_index("gx") * lax.axis_size("gy") + lax.axis_index("gy")
    first = lax.broadcasted_iota(jnp.int32, (TILES, TILES), 0)
    second = lax.broadcasted_iota(jnp.int32, (TILES, TILES), 1)
    before = jnp.where(first < second, 1.0, 0.0)
    ones = jnp.ones((8, TILES), F32)
    owned = jnp.where(owner_ref[...] == me, 1.0, 0.0)
    counts = lax.dot_general(ones, owned, (((1,), (1,)), ((), ())), preferred_element_type=F32)
    starts = jnp.dot(counts, before, preferred_element_type=F32)
    starts_v[...] = starts.astype(jnp.int32)
    starts_copy = pltpu.make_async_copy(starts_v, starts_ref, scalars.at[0])
    starts_copy.start()

    mine = jnp.broadcast_to(owner_ref[pl.ds(me, 1), :], (TILES, TILES)).astype(F32)
    column = mine.T
    rank = jnp.dot(ones, jnp.where(column == mine, before, 0.0), preferred_element_type=F32)
    per_owner = jnp.dot(ones, jnp.where(column == second.astype(F32), 1.0, 0.0), preferred_element_type=F32)
    lane = lane_ids().astype(F32)
    free = jnp.min(jnp.where(per_owner < 2.0, lane, 1000.0), axis=1, keepdims=True)
    mine = mine[:8]
    icy = mine < TILES
    slot = jnp.where(icy, 2.0 * mine + rank, 2.0 * free + 1.0)
    row = lax.broadcasted_iota(jnp.int32, (8, TILES), 0)
    pos_v[...] = jnp.where(row == 0, slot, jnp.where(icy, 1.0, 0.0)).astype(jnp.int32)
    pos_copy = pltpu.make_async_copy(pos_v, pos_ref, scalars.at[1])
    pos_copy.start()

    for n in range(4):
        loads[n].wait()
    chunk = lane_ids() // HALO

    def sea_edges(i):
        moved = []
        for half in range(2):
            rows = slice(8 * i + half * LANES, 8 * i + half * LANES + 8)
            for f, ref in enumerate((ou_ref, ov_ref, wx_ref, wy_ref)):
                moved.append(roll(ref[rows, :], (4 * half + f) * HALO))
        yield
        west, east = moved[0], moved[0]
        for n in range(1, 8):
            west = jnp.where(chunk == n, moved[n], west)
            east = jnp.where(chunk == n - 1, moved[n], east)
        west_ref[8 * i : 8 * i + 8, :] = west
        east_ref[8 * i : 8 * i + 8, :] = east

    interleave([sea_edges(i) for i in range(BANDS // 2)], 5)

    for n in range(6, 11):
        loads[n].wait()
    for g in range(SLOTS // 8):
        eight = slice(8 * g, 8 * g + 8)
        for h in range(2):
            cut = slice(h * LANES, (h + 1) * LANES)
            con = [con_ref[c, eight, cut] for c in range(5)]
            mass = sum(thk_ref[c, eight, cut] * con[c] for c in range(5))
            strength = mass * jnp.exp(-20.0 * (1.0 - sum(con)))
            rows = [str_ref[f, eight, cut] for f in range(3)]
            rows += [strength, mass, mask_ref[eight, cut].astype(F32)]
            for f, x in enumerate(rows):
                blk[pl.ds(128 * g + 8 * h + 2 + f, 8, stride=16), :] = x
            for j in range(8):
                at = 128 * g + 16 * j + 8 * h
                blk[at : at + 2, :] = vel_ref[8 * g + j, :, cut]

    loads[4].wait()
    starts_copy.wait()
    pos_copy.wait()
    for t in range(TILES):
        at = pl.multiple_of(starts_ref[0, t] * 16, 16)
        out_ref[2 * t] = blk[pl.ds(at, 16), :]
        out_ref[2 * t + 1] = blk[pl.ds(at + 16, 16), :]


def pack(owner_list, ice_mask, velocity, stress, thickness, concentration, maps):
    def by_field(x):
        return jnp.transpose(x, (1, 0, 2))

    inputs = (
        *maps, owner_list, by_field(concentration), by_field(thickness), by_field(stress), ice_mask, velocity
    )
    return pl.pallas_call(
        pack_kernel,
        in_specs=[pl.BlockSpec(memory_space=pltpu.HBM)] * 11,
        out_specs=[pl.BlockSpec(memory_space=pltpu.SMEM if n in (1, 2) else pltpu.VMEM) for n in range(10)],
        out_shape=(
            jax.ShapeDtypeStruct((2 * TILES, 2 * FIELDS, LANES), F32),
            pltpu.SMEM((8, TILES), jnp.int32),
            pltpu.SMEM((8, TILES), jnp.int32),
            jax.ShapeDtypeStruct((ROWS // 2, LANES), F32),
            jax.ShapeDtypeStruct((ROWS // 2, LANES), F32),
        )
        + (jax.ShapeDtypeStruct((ROWS, LANES), F32),) * 5,
        scratch_shapes=[pltpu.VMEM(x.shape, x.dtype) for x in inputs[5:]]
        + [
            pltpu.VMEM(((SLOTS + 8) * 16, LANES), F32),
            pltpu.VMEM((8, TILES), jnp.int32),
            pltpu.VMEM((8, TILES), jnp.int32),
            pltpu.SemaphoreType.DMA((2,)),
            pltpu.SemaphoreType.DMA((11,)),
        ],
        compiler_params=pltpu.CompilerParams(vmem_limit_bytes=VMEM_BYTES),
        name="pack",
    )(*(pltpu.with_memory_space_constraint(x, pltpu.HBM) for x in inputs))


def unpack_tile_kernel(pos_ref, recv_ref, temp_ref, sea_west_ref, sea_east_ref, tile_ref, west_ref, east_ref, room):
    chunk = lane_ids() // HALO

    def band(i):
        base = i * 64
        rows = slice(8 * i, 8 * i + 8)
        quads = []
        for h in range(2):
            four = []
            for k in range(4 * i, 4 * i + 4):
                got = recv_ref[pos_ref[0, k], h * FIELDS : (h + 1) * FIELDS, :]
                four.append(jnp.where(pos_ref[1, k] > 0, got, 0.0))
            quads.append(four)
        quads = yield from swap_chunks(quads, room.at[i])
        for h in range(2):
            for r, x in enumerate(quads[h]):
                tile_ref[pl.ds(base + h * 4 + r, FIELDS, stride=8), :] = x
        melt = jnp.exp(-0.5 * jnp.maximum(temp_ref[rows, :], 0.0))
        yield
        moved = []
        for f in range(FIELDS):
            at = slice(base + 8 * f, base + 8 * f + 8)
            x = tile_ref[at, :]
            if f == 5:
                x = x * melt
                tile_ref[at, :] = x
            moved.append(roll(x, f * HALO))
        yield
        west, east = moved[0], moved[0]
        for f in range(1, FIELDS):
            west = jnp.where(chunk == f, moved[f], west)
            east = jnp.where(chunk == f - 1, moved[f], east)
        west_ref[rows, :] = west
        east_ref[rows, :] = east

    interleave([band(i) for i in range(BANDS)], 12)
    west_ref[ROWS:, :] = sea_west_ref[...]
    east_ref[ROWS:, :] = sea_east_ref[...]


EDGE = ROWS + ROWS // 2


def unpack_tile(pos, recv, temp, sea_west, sea_east):
    return pl.pallas_call(
        unpack_tile_kernel,
        in_specs=specs(5),
        out_shape=(
            jax.ShapeDtypeStruct((BANDS * FIELDS * 8, LANES), F32),
            jax.ShapeDtypeStruct((EDGE, LANES), F32),
            jax.ShapeDtypeStruct((EDGE, LANES), F32),
        ),
        scratch_shapes=[pltpu.VMEM((BANDS, 2, 4, 8, LANES), F32)],
        compiler_params=pltpu.CompilerParams(vmem_limit_bytes=VMEM_BYTES),
        name="unpack_tile",
    )(pos, recv, temp, sea_west, sea_east)


STATE = ("u", "v", "p", "m", "t")
STATIC = ("ou", "ov", "wx", "wy", "inertia", "turn", "k", "cover")


def put_ice(s, i, ice, row_ids, grid_rows):
    u, v, total, diff, shear, strength, mass, cover = ice
    at = slice(8 + 8 * i, 16 + 8 * i)
    here = slice(8 * i, 8 * i + 8)
    s["u"][at, :] = u
    s["v"][at, :] = v
    s["p"][at, :] = (0.25 * cover) * (total + diff)
    s["m"][at, :] = (0.25 * cover) * (total - diff)
    s["t"][at, :] = (0.5 * cover) * shear
    coriolis = 2.0 * (row_ids.astype(F32) + 0.5) / grid_rows - 1.0
    s["inertia"][here, :] = 2.0 * mass
    s["turn"][here, :] = mass * coriolis
    s["k"][here, :] = (0.1 * I14) * (cover * strength)
    s["cover"][here, :] = cover


def put_ocean(s, i, ocean):
    here = slice(8 * i, 8 * i + 8)
    for name, x in zip(("ou", "ov", "wx", "wy"), ocean):
        s[name][here, :] = x


def clear_ends(s, chunks):
    zero = jnp.zeros((8, LANES), F32)
    for name in STATE:
        s[name][0:8, :] = zero
        s[name][8 + 8 * chunks : 16 + 8 * chunks, :] = zero


def run_subcycles(s, stress_chunks, velocity_chunks, times=1):
    def subcycle(step, carry):
        for i in stress_chunks:
            a = 8 + 8 * i
            at, up, down = slice(a, a + 8), slice(a + 1, a + 9), slice(a - 1, a + 7)
            here = slice(8 * i, 8 * i + 8)
            u, v = s["u"][at, :], s["v"][at, :]
            exx = roll(u, -1) - roll(u, 1)
            eyy = s["v"][up, :] - s["v"][down, :]
            shear = (s["u"][up, :] - s["u"][down, :]) + (roll(v, -1) - roll(v, 1))
            div = exx + eyy
            ten = exx - eyy
            ten4, shear4 = 0.25 * ten, 0.25 * shear
            q = div * div + (ten * ten4 + shear * shear4) + 0.04
            inv = lax.rsqrt(q)
            k = s["k"][here, :] * inv
            base = div - q * inv
            s["p"][at, :] = I14 * s["p"][at, :] + k * (base + ten4)
            s["m"][at, :] = I14 * s["m"][at, :] + k * (base - ten4)
            s["t"][at, :] = I14 * s["t"][at, :] + k * shear4
        for i in velocity_chunks:
            a = 8 + 8 * i
            at, up, down = slice(a, a + 8), slice(a + 1, a + 9), slice(a - 1, a + 7)
            here = slice(8 * i, 8 * i + 8)
            p, t = s["p"][at, :], s["t"][at, :]
            fx = (roll(p, -1) - roll(p, 1)) + (s["t"][up, :] - s["t"][down, :])
            fy = (roll(t, -1) - roll(t, 1)) + (s["m"][up, :] - s["m"][down, :])
            u, v = s["u"][at, :], s["v"][at, :]
            ou, ov = s["ou"][here, :], s["ov"][here, :]
            du, dv = ou - u, ov - v
            g = du * du + dv * dv + 0.01
            drag = g * lax.rsqrt(g)
            inertia, turn = s["inertia"][here, :], s["turn"][here, :]
            diag = inertia + drag
            rx = inertia * u + fx + s["wx"][here, :] + drag * ou
            ry = inertia * v + fy + s["wy"][here, :] + drag * ov
            w = s["cover"][here, :] / (diag * diag + turn * turn)
            s["u"][at, :] = w * (diag * rx + turn * ry)
            s["v"][at, :] = w * (diag * ry - turn * rx)
        return carry

    if times == 1:
        subcycle(0, 0)
    else:
        lax.fori_loop(0, times // 4, lambda n, c: [subcycle(n, c) for _ in range(4)][-1], 0)


def state_scratch(chunks):
    tall = pltpu.VMEM((8 * chunks + 16, LANES), F32)
    flat = pltpu.VMEM((8 * chunks, LANES), F32)
    return [tall] * len(STATE) + [flat] * len(STATIC)


def named(scratch):
    return dict(zip(STATE + STATIC, scratch))


def at_row(i):
    return lax.axis_index("gy") * ROWS + 8 * i + lax.broadcasted_iota(jnp.int32, (8, LANES), 0)


def chunk_of(tile_ref, i):
    return [tile_ref[i * 64 + f * 8 : i * 64 + f * 8 + 8, :] for f in range(FIELDS)]


def stresses(p, m, t):
    return 2.0 * (p + m), 2.0 * (p - m), 2.0 * t


def state_of(s, i):
    at = slice(8 + 8 * i, 16 + 8 * i)
    return [s[name][at, :] for name in STATE]


def inner_kernel(tile_ref, ou_ref, ov_ref, wx_ref, wy_ref, out_ref, *scratch):
    s = named(scratch)
    grid_rows = ROWS * lax.axis_size("gy")
    clear_ends(s, BANDS)
    for i in range(BANDS):
        put_ice(s, i, chunk_of(tile_ref, i), at_row(i), grid_rows)
        put_ocean(s, i, [ref[8 * i : 8 * i + 8, :] for ref in (ou_ref, ov_ref, wx_ref, wy_ref)])
    run_subcycles(s, range(BANDS), range(BANDS), SUBS)
    for i in range(BANDS):
        for f, x in enumerate(state_of(s, i)):
            out_ref[f, 8 * i : 8 * i + 8, :] = x


def inner(tile, ocean):
    return pl.pallas_call(
        inner_kernel,
        out_shape=jax.ShapeDtypeStruct((FINAL, ROWS, LANES), F32),
        scratch_shapes=state_scratch(BANDS),
        compiler_params=pltpu.CompilerParams(vmem_limit_bytes=VMEM_BYTES),
        cost_estimate=pl.CostEstimate(flops=4_000_000, bytes_accessed=4_000_000, transcendentals=800_000),
        name="inner",
    )(tile, *ocean)


def strip_moves(own, west, east, chunk):
    return own, roll(own, -32), roll(west, (8 - chunk) * HALO), roll(east, (6 - chunk) * HALO)


def strip(own, moved, west, east, lane):
    x = jnp.where(lane < 48, own, moved)
    x = jnp.where(lane >= 112, west, x)
    return jnp.where((lane >= 96) & (lane < 112), east, x)


def ice_strips(own, west, east, edge, lane):
    west = jnp.where(edge[0], 0.0, west)
    east = jnp.where(edge[1], 0.0, east)
    moved = [strip_moves(own[f], west, east, f) for f in range(FIELDS)]
    yield
    return [strip(*x, lane) for x in moved]


def ocean_strips(own, west, east, half, lane):
    moved = [strip_moves(own[f], west, east, 4 * half + f) for f in range(4)]
    yield
    return [strip(*x, lane) for x in moved]


def edges_x():
    a = lax.axis_index("gx")
    return a == 0, a == lax.axis_size("gx") - 1


def edges_y():
    b = lax.axis_index("gy")
    return b == 0, b == lax.axis_size("gy") - 1


def join(mid, strips, moved, lane):
    x = jnp.where(lane < HALO, strips, mid)
    return jnp.where(lane >= LANES - HALO, moved, x)


def finish_band(band, mids, strips, refs, drag_ref, stage, room, lane):
    pos_ref, tile_ref, ou_ref, ov_ref, packed_ref = refs
    moved = [roll(x, 32) for x in strips()]
    yield
    u, v, *pmt = [join(*x, lane) for x in zip(mids(), strips(), moved)]
    five = [u, v, *stresses(*pmt)]
    for f, x in enumerate(five):
        for h in range(2):
            at = h * 32 + f * 4
            stage[at : at + 4, :] = x[4 * h : 4 * h + 4, :]
    rows = slice(8 * band, 8 * band + 8)
    cover = tile_ref[band * 64 + 56 : band * 64 + 64, :]
    drag_ref[0], drag_ref[1] = drag_rows(five, ou_ref[rows, :], ov_ref[rows, :], cover)
    yield
    quads = [[stage[pl.ds(32 * h + r, 8, stride=4), :] for r in range(4)] for h in range(2)]
    quads = yield from swap_chunks(quads, room)
    for c in range(4):
        at = pos_ref[0, band * 4 + c] * 2 * FINAL
        for h in range(2):
            packed_ref[pl.ds(at + h * FINAL, FINAL), :] = quads[h][c][:FINAL]


def drag_rows(five, ou, ov, cover):
    du, dv = five[0] - ou, five[1] - ov
    g = du * du + dv * dv + 0.01
    drag = cover * (g * lax.rsqrt(g))
    return drag * du, drag * dv


def sides_kernel(
    pos_ref, tile_ref, west_ref, east_ref, ou_ref, ov_ref, wx_ref, wy_ref, mid_ref, packed_ref, drag_ref, stage, room, *scratch,
):
    s = named(scratch)
    lane = lane_ids()
    grid_rows = ROWS * lax.axis_size("gy")
    edge = edges_x()
    clear_ends(s, BANDS)

    def start(i):
        rows = slice(8 * i, 8 * i + 8)
        ice = yield from ice_strips(chunk_of(tile_ref, i), west_ref[rows, :], east_ref[rows, :], edge, lane)
        put_ice(s, i, ice, at_row(i), grid_rows)
        half, j = divmod(i, BANDS // 2)
        sea = slice(ROWS + 8 * j, ROWS + 8 * j + 8)
        own = [ref[rows, :] for ref in (ou_ref, ov_ref, wx_ref, wy_ref)]
        put_ocean(s, i, (yield from ocean_strips(own, west_ref[sea, :], east_ref[sea, :], half, lane)))

    interleave([start(i) for i in range(BANDS)], 3)
    run_subcycles(s, range(BANDS), range(BANDS), SUBS)
    refs = (pos_ref, tile_ref, ou_ref, ov_ref, packed_ref)

    def finish(i):
        def mids():
            return [mid_ref[f, 8 * i : 8 * i + 8, :] for f in range(FINAL)]

        drag = drag_ref.at[:, pl.ds(8 * i - HALO, 8), :]
        yield from finish_band(i, mids, lambda: state_of(s, i), refs, drag, stage.at[i], room.at[i], lane)

    interleave([finish(i) for i in range(2, BANDS - 2)], 8)


def stage_scratch(bands):
    return [pltpu.VMEM((bands, 64, LANES), F32), pltpu.VMEM((bands, 2, 4, 8, LANES), F32)]


def results(rows):
    return pltpu.VMEM((2 * TILES * 2 * FINAL, LANES), F32), jax.ShapeDtypeStruct((2, rows, LANES), F32)


def sides(pos, tile, west, east, ocean, mid):
    return pl.pallas_call(
        sides_kernel,
        in_specs=specs(9),
        out_shape=results(ROWS - 2 * HALO),
        out_specs=specs(3)[1:],
        scratch_shapes=stage_scratch(BANDS) + state_scratch(BANDS),
        compiler_params=pltpu.CompilerParams(vmem_limit_bytes=VMEM_BYTES),
        cost_estimate=pl.CostEstimate(flops=5_000_000, bytes_accessed=5_000_000, transcendentals=800_000),
        name="sides",
    )(pos, tile, west, east, *ocean, mid)


def ends_kernel(
    pos_ref, tile_ref, west_ref, east_ref, north_ref, south_ref, ou_ref, ov_ref, wx_ref, wy_ref,
    packed_in, packed_ref, drag_ref, stage, room, *scratch,
):
    del packed_in
    s = named(scratch)
    lane = lane_ids()
    grid_rows = ROWS * lax.axis_size("gy")
    edge = edges_x()
    outside = edges_y()
    ocean_refs = (ou_ref, ov_ref, wx_ref, wy_ref)
    clear_ends(s, 24)

    def start(end, j):
        ref = (north_ref, south_ref)[end]
        i = (j - 2) if end == 0 else BANDS - 4 + j
        half = 1 - end if not 0 <= i < BANDS else i // (BANDS // 2)
        if 0 <= i < BANDS:
            rows = slice(8 * i, 8 * i + 8)
            own = chunk_of(tile_ref, i)
            west, east = west_ref[rows, :], east_ref[rows, :]
            water = [x[rows, :] for x in ocean_refs]
            at = ROWS + 8 * (i % (BANDS // 2))
            sea_west, sea_east = west_ref[at : at + 8, :], east_ref[at : at + 8, :]
        else:
            at = 8 * (i % 2)

            def part_of(base):
                return ref[base + at : base + at + 8, :]

            own = [jnp.where(outside[end], 0.0, x) for x in chunk_of(ref, i % 2)]
            west = jnp.where(outside[end], 0.0, part_of(128))
            east = jnp.where(outside[end], 0.0, part_of(144))
            water = [part_of(160 + 16 * f) for f in range(4)]
            sea_west, sea_east = part_of(224), part_of(240)
        for part in range(2):
            chunk = part * 12 + end * 6 + j
            ice = (yield from ice_strips(own, west, east, edge, lane)) if part else own
            put_ice(s, chunk, ice, at_row(i), grid_rows)
            if part:
                water = yield from ocean_strips(water, sea_west, sea_east, half, lane)
            put_ocean(s, chunk, water)

    interleave([start(end, j) for end in range(2) for j in range(6)], 3)
    every = range(24)
    four = [c for c in every if c % 6 not in (0, 5)]
    two = [c for c in every if c % 6 in (2, 3)]
    for step in range(1, SUBS + 1):
        stress = every if step < 5 else four
        run_subcycles(s, stress, every if step < 4 else four if step < 8 else two)
    refs = (pos_ref, tile_ref, ou_ref, ov_ref, packed_ref)

    def finish(n):
        end, j = divmod(n, 2)
        chunk = end * 6 + j + 2
        i = BANDS - 2 + j if end else j
        drag = drag_ref.at[:, pl.ds(8 * n, 8), :]
        yield from finish_band(i, lambda: state_of(s, chunk), lambda: state_of(s, chunk + 12), refs, drag, stage.at[n], room.at[n], lane)

    interleave([finish(n) for n in range(4)], 4)


def ends(pos, tile, west, east, north, south, ocean, packed):
    packed = pltpu.with_memory_space_constraint(packed, pltpu.VMEM)
    return pl.pallas_call(
        ends_kernel,
        in_specs=specs(11),
        out_shape=results(2 * HALO),
        out_specs=specs(3)[1:],
        input_output_aliases={10: 0},
        scratch_shapes=stage_scratch(4) + state_scratch(24),
        compiler_params=pltpu.CompilerParams(vmem_limit_bytes=VMEM_BYTES),
        name="ends",
    )(pos, tile, west, east, north, south, *ocean, packed)


def unpack_ice_kernel(starts_ref, recv_ref, mid_ref, end_ref, vel_out, str_out, drag_out, blk, vel_ref, str_ref, sems):
    first, last = pl.ds(0, HALO), pl.ds(ROWS - HALO, HALO)
    copies = [
        pltpu.make_async_copy(mid_ref, drag_out.at[:, pl.ds(HALO, ROWS - 2 * HALO), :], sems.at[0]),
        pltpu.make_async_copy(end_ref.at[:, first, :], drag_out.at[:, first, :], sems.at[1]),
        pltpu.make_async_copy(end_ref.at[:, pl.ds(HALO, HALO), :], drag_out.at[:, last, :], sems.at[2]),
    ]
    for copy in copies:
        copy.start()
    for t in range(TILES):
        start = starts_ref[0, t]
        for c in range(2):
            at = (2 * t + c) * 2 * FINAL
            to = pl.multiple_of((start + c) * 16, 16)
            blk[pl.ds(to, 2 * FINAL), :] = recv_ref[at : at + 2 * FINAL, :]
    half = SLOTS // 2
    for part in range(2):
        for g in range(part * half // 8, (part + 1) * half // 8):
            eight = slice(8 * g, 8 * g + 8)
            for h in range(2):
                cut = slice(h * LANES, (h + 1) * LANES)
                for f in range(3):
                    str_ref[f, eight, cut] = blk[pl.ds(128 * g + h * FINAL + 2 + f, 8, stride=16), :]
                for j in range(8):
                    at = 128 * g + 16 * j + h * FINAL
                    vel_ref[8 * g + j, :, cut] = blk[at : at + 2, :]
        some = pl.ds(part * half, half)
        parts = [
            pltpu.make_async_copy(vel_ref.at[some], vel_out.at[some], sems.at[3 + 2 * part]),
            pltpu.make_async_copy(str_ref.at[:, some, :], str_out.at[:, some, :], sems.at[4 + 2 * part]),
        ]
        for copy in parts:
            copy.start()
        copies += parts
    for copy in copies:
        copy.wait()


def unpack_ice(starts, recv, drag_mid, drag_ends):
    vel_shape, str_shape = (SLOTS, 2, 2 * LANES), (3, SLOTS, 2 * LANES)
    vel, strs, drag = pl.pallas_call(
        unpack_ice_kernel,
        in_specs=specs(4),
        out_specs=[pl.BlockSpec(memory_space=pltpu.HBM)] * 3,
        out_shape=tuple(pltpu.HBM(shape, F32) for shape in (vel_shape, str_shape, (2, ROWS, LANES))),
        scratch_shapes=[
            pltpu.VMEM(((SLOTS + 8) * 16, LANES), F32),
            pltpu.VMEM(vel_shape, F32),
            pltpu.VMEM(str_shape, F32),
            pltpu.SemaphoreType.DMA((7,)),
        ],
        compiler_params=pltpu.CompilerParams(vmem_limit_bytes=VMEM_BYTES),
        name="unpack_ice",
    )(starts, recv, drag_mid, drag_ends)
    return vel, jnp.transpose(strs, (1, 0, 2)), drag


def both_ways(axis, forward, backward):
    n = lax.axis_size(axis)
    return (
        lax.ppermute(forward, axis, [(i, (i + 1) % n) for i in range(n)]),
        lax.ppermute(backward, axis, [((i + 1) % n, i) for i in range(n)]),
    )


def on_device(
    owner_list, ice_mask, velocity, stress, thickness, concentration, ocean_u, ocean_v, wind_x, wind_y, surface_temp
):
    ocean = (ocean_u, ocean_v, wind_x, wind_y)
    outbound, starts, pos, sea_west, sea_east, *maps = pack(
        owner_list, ice_mask, velocity, stress, thickness, concentration, (*ocean, surface_temp)
    )
    *ocean, surface_temp = maps
    arrived = lax.all_to_all(outbound, AXES, split_axis=0, concat_axis=0, tiled=True)
    tile, west_edge, east_edge = unpack_tile(pos, arrived, surface_temp, sea_west, sea_east)
    west, east = both_ways("gx", east_edge, west_edge)
    west, east, mid = lax.optimization_barrier((west, east, inner(tile, ocean)))

    def edge(cells, block_rows, sea_rows):
        parts = [tile[block_rows], west[:ROWS][cells], east[:ROWS][cells]]
        parts += [x[cells] for x in ocean] + [west[sea_rows], east[sea_rows]]
        return jnp.concatenate(parts, axis=0)

    low = edge(slice(0, HALO), slice(0, 128), slice(ROWS, ROWS + HALO))
    high = edge(slice(ROWS - HALO, ROWS), slice(-128, None), slice(EDGE - HALO, EDGE))
    north, south = both_ways("gy", high, low)
    packed, drag_mid = sides(pos, tile, west, east, ocean, mid)
    packed, drag_ends = ends(pos, tile, west, east, north, south, ocean, packed)

    homeward = packed.reshape(2 * TILES, FINAL, 2, LANES)
    back = lax.all_to_all(homeward, AXES, split_axis=0, concat_axis=0, tiled=True)
    return unpack_ice(starts, back.reshape(2 * TILES * 2 * FINAL, LANES), drag_mid, drag_ends)


def solution(mesh):
    blocks = P(AXES, None, None)
    return jax.shard_map(
        on_device,
        mesh=mesh,
        in_specs=(P(), P(AXES, None)) + (blocks,) * 4 + (P("gy", "gx"),) * 5,
        out_specs=(blocks, blocks, P(None, "gy", "gx")),
        check_vma=False,
    )
```

```python
import jax
import jax.numpy as jnp
from jax import lax
from jax.experimental import pallas as pl
from jax.experimental.pallas import tpu as pltpu
from jax.sharding import PartitionSpec as P

AXES = ("gx", "gy")
TILES = 128
SLOTS = 112
ROWS = 256
LANES = 128
BANDS = ROWS // 8
HALO = 16
SUBS = 8
FIELDS = 8
FINAL = 5
I14 = 1.0 / 1.4
F32 = jnp.float32
VMEM_BYTES = 24 * 1024 * 1024


def specs(count):
    return [pl.BlockSpec(memory_space=pltpu.SMEM)] + [pl.BlockSpec(memory_space=pltpu.VMEM)] * (count - 1)


def lane_ids(rows=8):
    return lax.broadcasted_iota(jnp.int32, (rows, LANES), 1)


def roll(x, shift):
    return pltpu.roll(x, shift % LANES, 1) if shift % LANES else x


def interleave(tasks, width):
    tasks = list(tasks)
    active = []
    while tasks or active:
        if tasks and len(active) < width:
            active.append(tasks.pop(0))
        running = []
        for task in active:
            try:
                next(task)
                running.append(task)
            except StopIteration:
                pass
        active = running


def swap_chunks(quads, room):
    chunk = lane_ids() // 32
    moved = [[roll(x, 32 * c) for c, x in enumerate(quad)] for quad in quads]
    yield
    for q, quad in enumerate(moved):
        for c, x in enumerate(quad):
            room[q, c] = x
    yield
    out = []
    for q in range(len(quads)):
        kept = [room[q, c] for c in range(4)]
        rows = []
        for r in range(4):
            x = kept[-r % 4]
            for to in range(1, 4):
                x = jnp.where(chunk == to, kept[(to - r) % 4], x)
            rows.append(roll(x, -32 * r))
        out.append(rows)
    yield
    return out


def pack_kernel(*refs):
    far, refs = refs[:11], refs[11:]
    (out_ref, starts_ref, pos_ref, west_ref, east_ref), refs = refs[:5], refs[5:]
    here, (blk, starts_v, pos_v, scalars, sems) = refs[:11], refs[11:]
    ou_ref, ov_ref, wx_ref, wy_ref, _, owner_ref, con_ref, thk_ref, str_ref, mask_ref, vel_ref = here
    loads = [pltpu.make_async_copy(x, y, sems.at[n]) for n, (x, y) in enumerate(zip(far, here))]
    for n in (5, 0, 1, 2, 3, 6, 7, 8, 9, 10, 4):
        loads[n].start()
    loads[5].wait()
    me = lax.axis_index("gx") * lax.axis_size("gy") + lax.axis_index("gy")
    first = lax.broadcasted_iota(jnp.int32, (TILES, TILES), 0)
    second = lax.broadcasted_iota(jnp.int32, (TILES, TILES), 1)
    before = jnp.where(first < second, 1.0, 0.0)
    ones = jnp.ones((8, TILES), F32)
    owned = jnp.where(owner_ref[...] == me, 1.0, 0.0)
    counts = lax.dot_general(ones, owned, (((1,), (1,)), ((), ())), preferred_element_type=F32)
    starts = jnp.dot(counts, before, preferred_element_type=F32)
    starts_v[...] = starts.astype(jnp.int32)
    starts_copy = pltpu.make_async_copy(starts_v, starts_ref, scalars.at[0])
    starts_copy.start()

    mine = jnp.broadcast_to(owner_ref[pl.ds(me, 1), :], (TILES, TILES)).astype(F32)
    column = mine.T
    rank = jnp.dot(ones, jnp.where(column == mine, before, 0.0), preferred_element_type=F32)
    per_owner = jnp.dot(ones, jnp.where(column == second.astype(F32), 1.0, 0.0), preferred_element_type=F32)
    lane = lane_ids().astype(F32)
    free = jnp.min(jnp.where(per_owner < 2.0, lane, 1000.0), axis=1, keepdims=True)
    mine = mine[:8]
    icy = mine < TILES
    slot = jnp.where(icy, 2.0 * mine + rank, 2.0 * free + 1.0)
    row = lax.broadcasted_iota(jnp.int32, (8, TILES), 0)
    pos_v[...] = jnp.where(row == 0, slot, jnp.where(icy, 1.0, 0.0)).astype(jnp.int32)
    pos_copy = pltpu.make_async_copy(pos_v, pos_ref, scalars.at[1])
    pos_copy.start()

    for n in range(4):
        loads[n].wait()
    chunk = lane_ids() // HALO

    def sea_edges(i):
        moved = []
        for half in range(2):
            rows = slice(8 * i + half * LANES, 8 * i + half * LANES + 8)
            for f, ref in enumerate((ou_ref, ov_ref, wx_ref, wy_ref)):
                moved.append(roll(ref[rows, :], (4 * half + f) * HALO))
        yield
        west, east = moved[0], moved[0]
        for n in range(1, 8):
            west = jnp.where(chunk == n, moved[n], west)
            east = jnp.where(chunk == n - 1, moved[n], east)
        west_ref[8 * i : 8 * i + 8, :] = west
        east_ref[8 * i : 8 * i + 8, :] = east

    interleave([sea_edges(i) for i in range(BANDS // 2)], 5)

    for n in range(6, 11):
        loads[n].wait()
    for g in range(SLOTS // 8):
        eight = slice(8 * g, 8 * g + 8)
        for h in range(2):
            cut = slice(h * LANES, (h + 1) * LANES)
            con = [con_ref[c, eight, cut] for c in range(5)]
            mass = sum(thk_ref[c, eight, cut] * con[c] for c in range(5))
            strength = mass * jnp.exp(-20.0 * (1.0 - sum(con)))
            rows = [str_ref[f, eight, cut] for f in range(3)]
            rows += [strength, mass, mask_ref[eight, cut].astype(F32)]
            for f, x in enumerate(rows):
                blk[pl.ds(128 * g + 8 * h + 2 + f, 8, stride=16), :] = x
            for j in range(8):
                at = 128 * g + 16 * j + 8 * h
                blk[at : at + 2, :] = vel_ref[8 * g + j, :, cut]

    loads[4].wait()
    starts_copy.wait()
    pos_copy.wait()
    for t in range(TILES):
        at = pl.multiple_of(starts_ref[0, t] * 16, 16)
        out_ref[2 * t] = blk[pl.ds(at, 16), :]
        out_ref[2 * t + 1] = blk[pl.ds(at + 16, 16), :]


def pack(owner_list, ice_mask, velocity, stress, thickness, concentration, maps):
    def by_field(x):
        return jnp.transpose(x, (1, 0, 2))

    inputs = (
        *maps, owner_list, by_field(concentration), by_field(thickness), by_field(stress), ice_mask, velocity
    )
    return pl.pallas_call(
        pack_kernel,
        in_specs=[pl.BlockSpec(memory_space=pltpu.HBM)] * 11,
        out_specs=[pl.BlockSpec(memory_space=pltpu.SMEM if n in (1, 2) else pltpu.VMEM) for n in range(10)],
        out_shape=(
            jax.ShapeDtypeStruct((2 * TILES, 2 * FIELDS, LANES), F32),
            pltpu.SMEM((8, TILES), jnp.int32),
            pltpu.SMEM((8, TILES), jnp.int32),
            jax.ShapeDtypeStruct((ROWS // 2, LANES), F32),
            jax.ShapeDtypeStruct((ROWS // 2, LANES), F32),
        )
        + (jax.ShapeDtypeStruct((ROWS, LANES), F32),) * 5,
        scratch_shapes=[pltpu.VMEM(x.shape, x.dtype) for x in inputs[5:]]
        + [
            pltpu.VMEM(((SLOTS + 8) * 16, LANES), F32),
            pltpu.VMEM((8, TILES), jnp.int32),
            pltpu.VMEM((8, TILES), jnp.int32),
            pltpu.SemaphoreType.DMA((2,)),
            pltpu.SemaphoreType.DMA((11,)),
        ],
        compiler_params=pltpu.CompilerParams(vmem_limit_bytes=VMEM_BYTES),
        name="pack",
    )(*(pltpu.with_memory_space_constraint(x, pltpu.HBM) for x in inputs))


def by_parity(axis, up, down):
    even = lax.axis_index(axis) % 2 == 0
    return jnp.where(even, up, down), jnp.where(even, down, up)


def unpack_tile_kernel(pos_ref, recv_ref, temp_ref, sea_west_ref, sea_east_ref, tile_ref, near_ref, far_ref, even_ref, room):
    even_ref[...] = by_parity("gy", jnp.ones((8, LANES), F32), jnp.zeros((8, LANES), F32))[0]
    chunk = lane_ids() // HALO

    def band(i):
        base = i * 64
        rows = slice(8 * i, 8 * i + 8)
        quads = []
        for h in range(2):
            four = []
            for k in range(4 * i, 4 * i + 4):
                got = recv_ref[pos_ref[0, k], h * FIELDS : (h + 1) * FIELDS, :]
                four.append(jnp.where(pos_ref[1, k] > 0, got, 0.0))
            quads.append(four)
        quads = yield from swap_chunks(quads, room.at[i])
        for h in range(2):
            for r, x in enumerate(quads[h]):
                tile_ref[pl.ds(base + h * 4 + r, FIELDS, stride=8), :] = x
        melt = jnp.exp(-0.5 * jnp.maximum(temp_ref[rows, :], 0.0))
        yield
        moved = []
        for f in range(FIELDS):
            at = slice(base + 8 * f, base + 8 * f + 8)
            x = tile_ref[at, :]
            if f == 5:
                x = x * melt
                tile_ref[at, :] = x
            moved.append(roll(x, f * HALO))
        yield
        west, east = moved[0], moved[0]
        for f in range(1, FIELDS):
            west = jnp.where(chunk == f, moved[f], west)
            east = jnp.where(chunk == f - 1, moved[f], east)
        near_ref[rows, :], far_ref[rows, :] = by_parity("gx", east, west)

    interleave([band(i) for i in range(BANDS)], 12)
    near_ref[ROWS:, :], far_ref[ROWS:, :] = by_parity("gx", sea_east_ref[...], sea_west_ref[...])


EDGE = ROWS + ROWS // 2


def unpack_tile(pos, recv, temp, sea_west, sea_east):
    return pl.pallas_call(
        unpack_tile_kernel,
        in_specs=specs(5),
        out_shape=(
            jax.ShapeDtypeStruct((BANDS * FIELDS * 8, LANES), F32),
            jax.ShapeDtypeStruct((EDGE, LANES), F32),
            jax.ShapeDtypeStruct((EDGE, LANES), F32),
            jax.ShapeDtypeStruct((8, LANES), F32),
        ),
        scratch_shapes=[pltpu.VMEM((BANDS, 2, 4, 8, LANES), F32)],
        compiler_params=pltpu.CompilerParams(vmem_limit_bytes=VMEM_BYTES),
        name="unpack_tile",
    )(pos, recv, temp, sea_west, sea_east)


STATE = ("u", "v", "p", "m", "t")
STATIC = ("ou", "ov", "wx", "wy", "inertia", "turn", "k", "cover")


def put_ice(s, i, ice, row_ids, grid_rows):
    u, v, total, diff, shear, strength, mass, cover = ice
    at = slice(8 + 8 * i, 16 + 8 * i)
    here = slice(8 * i, 8 * i + 8)
    s["u"][at, :] = u
    s["v"][at, :] = v
    s["p"][at, :] = (0.25 * cover) * (total + diff)
    s["m"][at, :] = (0.25 * cover) * (total - diff)
    s["t"][at, :] = (0.5 * cover) * shear
    coriolis = 2.0 * (row_ids.astype(F32) + 0.5) / grid_rows - 1.0
    s["inertia"][here, :] = 2.0 * mass
    s["turn"][here, :] = mass * coriolis
    s["k"][here, :] = (0.1 * I14) * (cover * strength)
    s["cover"][here, :] = cover


def put_ocean(s, i, ocean):
    here = slice(8 * i, 8 * i + 8)
    for name, x in zip(("ou", "ov", "wx", "wy"), ocean):
        s[name][here, :] = x


def clear_ends(s, chunks):
    zero = jnp.zeros((8, LANES), F32)
    for name in STATE:
        s[name][0:8, :] = zero
        s[name][8 + 8 * chunks : 16 + 8 * chunks, :] = zero


def run_subcycles(s, stress_chunks, velocity_chunks, times=1):
    def subcycle(step, carry):
        for i in stress_chunks:
            a = 8 + 8 * i
            at, up, down = slice(a, a + 8), slice(a + 1, a + 9), slice(a - 1, a + 7)
            here = slice(8 * i, 8 * i + 8)
            u, v = s["u"][at, :], s["v"][at, :]
            exx = roll(u, -1) - roll(u, 1)
            eyy = s["v"][up, :] - s["v"][down, :]
            shear = (s["u"][up, :] - s["u"][down, :]) + (roll(v, -1) - roll(v, 1))
            div = exx + eyy
            ten = exx - eyy
            ten4, shear4 = 0.25 * ten, 0.25 * shear
            q = div * div + (ten * ten4 + shear * shear4) + 0.04
            inv = lax.rsqrt(q)
            k = s["k"][here, :] * inv
            base = div - q * inv
            s["p"][at, :] = I14 * s["p"][at, :] + k * (base + ten4)
            s["m"][at, :] = I14 * s["m"][at, :] + k * (base - ten4)
            s["t"][at, :] = I14 * s["t"][at, :] + k * shear4
        for i in velocity_chunks:
            a = 8 + 8 * i
            at, up, down = slice(a, a + 8), slice(a + 1, a + 9), slice(a - 1, a + 7)
            here = slice(8 * i, 8 * i + 8)
            p, t = s["p"][at, :], s["t"][at, :]
            fx = (roll(p, -1) - roll(p, 1)) + (s["t"][up, :] - s["t"][down, :])
            fy = (roll(t, -1) - roll(t, 1)) + (s["m"][up, :] - s["m"][down, :])
            u, v = s["u"][at, :], s["v"][at, :]
            ou, ov = s["ou"][here, :], s["ov"][here, :]
            du, dv = ou - u, ov - v
            g = du * du + dv * dv + 0.01
            drag = g * lax.rsqrt(g)
            inertia, turn = s["inertia"][here, :], s["turn"][here, :]
            diag = inertia + drag
            rx = inertia * u + fx + s["wx"][here, :] + drag * ou
            ry = inertia * v + fy + s["wy"][here, :] + drag * ov
            w = s["cover"][here, :] / (diag * diag + turn * turn)
            s["u"][at, :] = w * (diag * rx + turn * ry)
            s["v"][at, :] = w * (diag * ry - turn * rx)
        return carry

    if times == 1:
        subcycle(0, 0)
    else:
        lax.fori_loop(0, times // 4, lambda n, c: [subcycle(n, c) for _ in range(4)][-1], 0)


def state_scratch(chunks):
    tall = pltpu.VMEM((8 * chunks + 16, LANES), F32)
    flat = pltpu.VMEM((8 * chunks, LANES), F32)
    return [tall] * len(STATE) + [flat] * len(STATIC)


def named(scratch):
    return dict(zip(STATE + STATIC, scratch))


def at_row(i):
    return lax.axis_index("gy") * ROWS + 8 * i + lax.broadcasted_iota(jnp.int32, (8, LANES), 0)


def chunk_of(tile_ref, i):
    return [tile_ref[i * 64 + f * 8 : i * 64 + f * 8 + 8, :] for f in range(FIELDS)]


def stresses(p, m, t):
    return 2.0 * (p + m), 2.0 * (p - m), 2.0 * t


def state_of(s, i):
    at = slice(8 + 8 * i, 16 + 8 * i)
    return [s[name][at, :] for name in STATE]


def inner_kernel(tile_ref, ou_ref, ov_ref, wx_ref, wy_ref, out_ref, *scratch):
    s = named(scratch)
    grid_rows = ROWS * lax.axis_size("gy")
    clear_ends(s, BANDS)
    for i in range(BANDS):
        put_ice(s, i, chunk_of(tile_ref, i), at_row(i), grid_rows)
        put_ocean(s, i, [ref[8 * i : 8 * i + 8, :] for ref in (ou_ref, ov_ref, wx_ref, wy_ref)])
    run_subcycles(s, range(BANDS), range(BANDS), SUBS)
    for i in range(BANDS):
        for f, x in enumerate(state_of(s, i)):
            out_ref[f, 8 * i : 8 * i + 8, :] = x


def inner(tile, ocean):
    return pl.pallas_call(
        inner_kernel,
        out_shape=jax.ShapeDtypeStruct((FINAL, ROWS, LANES), F32),
        scratch_shapes=state_scratch(BANDS),
        compiler_params=pltpu.CompilerParams(vmem_limit_bytes=VMEM_BYTES),
        cost_estimate=pl.CostEstimate(flops=4_000_000, bytes_accessed=4_000_000, transcendentals=800_000),
        name="inner",
    )(tile, *ocean)


def strip_moves(own, west, east, chunk):
    return own, roll(own, -32), roll(west, (8 - chunk) * HALO), roll(east, (6 - chunk) * HALO)


def strip(own, moved, west, east, lane):
    x = jnp.where(lane < 48, own, moved)
    x = jnp.where(lane >= 112, west, x)
    return jnp.where((lane >= 96) & (lane < 112), east, x)


def ice_strips(own, west, east, edge, lane):
    west = jnp.where(edge[0], 0.0, west)
    east = jnp.where(edge[1], 0.0, east)
    moved = [strip_moves(own[f], west, east, f) for f in range(FIELDS)]
    yield
    return [strip(*x, lane) for x in moved]


def ocean_strips(own, west, east, half, lane):
    moved = [strip_moves(own[f], west, east, 4 * half + f) for f in range(4)]
    yield
    return [strip(*x, lane) for x in moved]


def edges_x():
    a = lax.axis_index("gx")
    return a == 0, a == lax.axis_size("gx") - 1


def edges_y():
    b = lax.axis_index("gy")
    return b == 0, b == lax.axis_size("gy") - 1


def join(mid, strips, moved, lane):
    x = jnp.where(lane < HALO, strips, mid)
    return jnp.where(lane >= LANES - HALO, moved, x)


def finish_band(band, mids, strips, refs, drag_ref, stage, room, lane):
    pos_ref, tile_ref, ou_ref, ov_ref, packed_ref = refs
    moved = [roll(x, 32) for x in strips()]
    yield
    u, v, *pmt = [join(*x, lane) for x in zip(mids(), strips(), moved)]
    five = [u, v, *stresses(*pmt)]
    for f, x in enumerate(five):
        for h in range(2):
            at = h * 32 + f * 4
            stage[at : at + 4, :] = x[4 * h : 4 * h + 4, :]
    rows = slice(8 * band, 8 * band + 8)
    cover = tile_ref[band * 64 + 56 : band * 64 + 64, :]
    drag_ref[0], drag_ref[1] = drag_rows(five, ou_ref[rows, :], ov_ref[rows, :], cover)
    yield
    quads = [[stage[pl.ds(32 * h + r, 8, stride=4), :] for r in range(4)] for h in range(2)]
    quads = yield from swap_chunks(quads, room)
    for c in range(4):
        at = pos_ref[0, band * 4 + c] * 2 * FINAL
        for h in range(2):
            packed_ref[pl.ds(at + h * FINAL, FINAL), :] = quads[h][c][:FINAL]


def drag_rows(five, ou, ov, cover):
    du, dv = five[0] - ou, five[1] - ov
    g = du * du + dv * dv + 0.01
    drag = cover * (g * lax.rsqrt(g))
    return drag * du, drag * dv


def sides_kernel(
    pos_ref, tile_ref, near_ref, far_ref, ou_ref, ov_ref, wx_ref, wy_ref, mid_ref, packed_ref, drag_ref, stage, room, *scratch,
):
    s = named(scratch)
    lane = lane_ids()
    grid_rows = ROWS * lax.axis_size("gy")
    edge = edges_x()
    clear_ends(s, BANDS)

    def start(i):
        rows = slice(8 * i, 8 * i + 8)
        east, west = by_parity("gx", near_ref[rows, :], far_ref[rows, :])
        ice = yield from ice_strips(chunk_of(tile_ref, i), west, east, edge, lane)
        put_ice(s, i, ice, at_row(i), grid_rows)
        half, j = divmod(i, BANDS // 2)
        sea = slice(ROWS + 8 * j, ROWS + 8 * j + 8)
        own = [ref[rows, :] for ref in (ou_ref, ov_ref, wx_ref, wy_ref)]
        east, west = by_parity("gx", near_ref[sea, :], far_ref[sea, :])
        put_ocean(s, i, (yield from ocean_strips(own, west, east, half, lane)))

    interleave([start(i) for i in range(BANDS)], 3)
    run_subcycles(s, range(BANDS), range(BANDS), SUBS)
    refs = (pos_ref, tile_ref, ou_ref, ov_ref, packed_ref)

    def finish(i):
        def mids():
            return [mid_ref[f, 8 * i : 8 * i + 8, :] for f in range(FINAL)]

        drag = drag_ref.at[:, pl.ds(8 * i - HALO, 8), :]
        yield from finish_band(i, mids, lambda: state_of(s, i), refs, drag, stage.at[i], room.at[i], lane)

    interleave([finish(i) for i in range(2, BANDS - 2)], 8)


def stage_scratch(bands):
    return [pltpu.VMEM((bands, 64, LANES), F32), pltpu.VMEM((bands, 2, 4, 8, LANES), F32)]


def results(rows):
    return pltpu.VMEM((2 * TILES * 2 * FINAL, LANES), F32), jax.ShapeDtypeStruct((2, rows, LANES), F32)


def sides(pos, tile, west, east, ocean, mid):
    return pl.pallas_call(
        sides_kernel,
        in_specs=specs(9),
        out_shape=results(ROWS - 2 * HALO),
        out_specs=specs(3)[1:],
        scratch_shapes=stage_scratch(BANDS) + state_scratch(BANDS),
        compiler_params=pltpu.CompilerParams(vmem_limit_bytes=VMEM_BYTES),
        cost_estimate=pl.CostEstimate(flops=5_000_000, bytes_accessed=5_000_000, transcendentals=800_000),
        name="sides",
    )(pos, tile, west, east, *ocean, mid)


def ends_kernel(
    pos_ref, tile_ref, near_ref, far_ref, inner_ref, outer_ref, ou_ref, ov_ref, wx_ref, wy_ref,
    packed_in, packed_ref, drag_ref, stage, room, *scratch,
):
    del packed_in
    s = named(scratch)
    lane = lane_ids()
    grid_rows = ROWS * lax.axis_size("gy")
    edge = edges_x()
    outside = edges_y()
    ocean_refs = (ou_ref, ov_ref, wx_ref, wy_ref)
    clear_ends(s, 24)

    def start(end, j):
        i = (j - 2) if end == 0 else BANDS - 4 + j
        half = 1 - end if not 0 <= i < BANDS else i // (BANDS // 2)
        if 0 <= i < BANDS:
            rows = slice(8 * i, 8 * i + 8)
            own = chunk_of(tile_ref, i)
            east, west = by_parity("gx", near_ref[rows, :], far_ref[rows, :])
            water = [x[rows, :] for x in ocean_refs]
            at = ROWS + 8 * (i % (BANDS // 2))
            sea_east, sea_west = by_parity("gx", near_ref[at : at + 8, :], far_ref[at : at + 8, :])
        else:
            at = 8 * (i % 2)

            def part_of(base):
                rows = slice(base, base + 8)
                south, north = by_parity("gy", inner_ref[rows, :], outer_ref[rows, :])
                return south if end else north

            own = [jnp.where(outside[end], 0.0, part_of(i % 2 * 64 + 8 * f)) for f in range(FIELDS)]
            east, west = by_parity("gx", part_of(128 + at), part_of(144 + at))
            west, east = jnp.where(outside[end], 0.0, west), jnp.where(outside[end], 0.0, east)
            water = [part_of(160 + 16 * f + at) for f in range(4)]
            sea_east, sea_west = by_parity("gx", part_of(224 + at), part_of(240 + at))
        for part in range(2):
            chunk = part * 12 + end * 6 + j
            ice = (yield from ice_strips(own, west, east, edge, lane)) if part else own
            put_ice(s, chunk, ice, at_row(i), grid_rows)
            if part:
                water = yield from ocean_strips(water, sea_west, sea_east, half, lane)
            put_ocean(s, chunk, water)

    interleave([start(end, j) for end in range(2) for j in range(6)], 3)
    every = range(24)
    four = [c for c in every if c % 6 not in (0, 5)]
    two = [c for c in every if c % 6 in (2, 3)]
    for step in range(1, SUBS + 1):
        stress = every if step < 5 else four
        run_subcycles(s, stress, every if step < 4 else four if step < 8 else two)
    refs = (pos_ref, tile_ref, ou_ref, ov_ref, packed_ref)

    def finish(n):
        end, j = divmod(n, 2)
        chunk = end * 6 + j + 2
        i = BANDS - 2 + j if end else j
        drag = drag_ref.at[:, pl.ds(8 * n, 8), :]
        yield from finish_band(i, lambda: state_of(s, chunk), lambda: state_of(s, chunk + 12), refs, drag, stage.at[n], room.at[n], lane)

    interleave([finish(n) for n in range(4)], 4)


def ends(pos, tile, west, east, north, south, ocean, packed):
    packed = pltpu.with_memory_space_constraint(packed, pltpu.VMEM)
    return pl.pallas_call(
        ends_kernel,
        in_specs=specs(11),
        out_shape=results(2 * HALO),
        out_specs=specs(3)[1:],
        input_output_aliases={10: 0},
        scratch_shapes=stage_scratch(4) + state_scratch(24),
        compiler_params=pltpu.CompilerParams(vmem_limit_bytes=VMEM_BYTES),
        name="ends",
    )(pos, tile, west, east, north, south, *ocean, packed)


def unpack_ice_kernel(starts_ref, recv_ref, mid_ref, end_ref, vel_out, str_out, drag_out, blk, vel_ref, str_ref, sems):
    first, last = pl.ds(0, HALO), pl.ds(ROWS - HALO, HALO)
    copies = [
        pltpu.make_async_copy(mid_ref, drag_out.at[:, pl.ds(HALO, ROWS - 2 * HALO), :], sems.at[0]),
        pltpu.make_async_copy(end_ref.at[:, first, :], drag_out.at[:, first, :], sems.at[1]),
        pltpu.make_async_copy(end_ref.at[:, pl.ds(HALO, HALO), :], drag_out.at[:, last, :], sems.at[2]),
    ]
    for copy in copies:
        copy.start()
    for t in range(TILES):
        start = starts_ref[0, t]
        for c in range(2):
            at = (2 * t + c) * 2 * FINAL
            to = pl.multiple_of((start + c) * 16, 16)
            blk[pl.ds(to, 2 * FINAL), :] = recv_ref[at : at + 2 * FINAL, :]
    half = SLOTS // 2
    for part in range(2):
        for g in range(part * half // 8, (part + 1) * half // 8):
            eight = slice(8 * g, 8 * g + 8)
            for h in range(2):
                cut = slice(h * LANES, (h + 1) * LANES)
                for f in range(3):
                    str_ref[f, eight, cut] = blk[pl.ds(128 * g + h * FINAL + 2 + f, 8, stride=16), :]
                for j in range(8):
                    at = 128 * g + 16 * j + h * FINAL
                    vel_ref[8 * g + j, :, cut] = blk[at : at + 2, :]
        some = pl.ds(part * half, half)
        parts = [
            pltpu.make_async_copy(vel_ref.at[some], vel_out.at[some], sems.at[3 + 2 * part]),
            pltpu.make_async_copy(str_ref.at[:, some, :], str_out.at[:, some, :], sems.at[4 + 2 * part]),
        ]
        for copy in parts:
            copy.start()
        copies += parts
    for copy in copies:
        copy.wait()


def unpack_ice(starts, recv, drag_mid, drag_ends):
    vel_shape, str_shape = (SLOTS, 2, 2 * LANES), (3, SLOTS, 2 * LANES)
    vel, strs, drag = pl.pallas_call(
        unpack_ice_kernel,
        in_specs=specs(4),
        out_specs=[pl.BlockSpec(memory_space=pltpu.HBM)] * 3,
        out_shape=tuple(pltpu.HBM(shape, F32) for shape in (vel_shape, str_shape, (2, ROWS, LANES))),
        scratch_shapes=[
            pltpu.VMEM(((SLOTS + 8) * 16, LANES), F32),
            pltpu.VMEM(vel_shape, F32),
            pltpu.VMEM(str_shape, F32),
            pltpu.SemaphoreType.DMA((7,)),
        ],
        compiler_params=pltpu.CompilerParams(vmem_limit_bytes=VMEM_BYTES),
        name="unpack_ice",
    )(starts, recv, drag_mid, drag_ends)
    return vel, jnp.transpose(strs, (1, 0, 2)), drag


def exchange(axis, near, far):
    nx, ny = lax.axis_size("gx"), lax.axis_size("gy")
    swaps = ([], [])
    for a in range(nx):
        for b in range(ny):
            at, n = (a, nx) if axis == "gx" else (b, ny)
            for swap, step in zip(swaps, (1 - at % 2 * 2, at % 2 * 2 - 1)):
                to = (a + step, b) if axis == "gx" else (a, b + step)
                if not 0 <= at + step < n:
                    to = (a, b ^ 1) if axis == "gx" else (a ^ 1, b)
                swap.append((a * ny + b, to[0] * ny + to[1]))
    far = lax.ppermute(far, AXES, swaps[1])
    return lax.ppermute(near, AXES, swaps[0]), far


def on_device(
    owner_list, ice_mask, velocity, stress, thickness, concentration, ocean_u, ocean_v, wind_x, wind_y, surface_temp
):
    ocean = (ocean_u, ocean_v, wind_x, wind_y)
    outbound, starts, pos, sea_west, sea_east, *maps = pack(
        owner_list, ice_mask, velocity, stress, thickness, concentration, (*ocean, surface_temp)
    )
    *ocean, surface_temp = maps
    arrived = lax.all_to_all(outbound, AXES, split_axis=0, concat_axis=0, tiled=True)
    tile, near, far, even = unpack_tile(pos, arrived, surface_temp, sea_west, sea_east)
    near, far = exchange("gx", near, far)
    near, far, mid, *ocean = lax.optimization_barrier((near, far, inner(tile, ocean), *ocean))

    def edge(cells, block_rows, sea_rows):
        parts = [tile[block_rows], near[:ROWS][cells], far[:ROWS][cells]]
        parts += [x[cells] for x in ocean] + [near[sea_rows], far[sea_rows]]
        return jnp.concatenate(parts, axis=0)

    low = edge(slice(0, HALO), slice(0, 128), slice(ROWS, ROWS + HALO))
    high = edge(slice(ROWS - HALO, ROWS), slice(-128, None), slice(EDGE - HALO, EDGE))
    even = even[:1] > 0.5
    near_y, far_y = exchange("gy", jnp.where(even, high, low), jnp.where(even, low, high))
    packed, drag_mid = sides(pos, tile, near, far, ocean, mid)
    packed, drag_ends = ends(pos, tile, near, far, near_y, far_y, ocean, packed)

    homeward = packed.reshape(2 * TILES, FINAL, 2, LANES)
    back = lax.all_to_all(homeward, AXES, split_axis=0, concat_axis=0, tiled=True)
    return unpack_ice(starts, back.reshape(2 * TILES * 2 * FINAL, LANES), drag_mid, drag_ends)


def solution(mesh):
    blocks = P(AXES, None, None)
    return jax.shard_map(
        on_device,
        mesh=mesh,
        in_specs=(P(), P(AXES, None)) + (blocks,) * 4 + (P("gy", "gx"),) * 5,
        out_specs=(blocks, blocks, P(None, "gy", "gx")),
        check_vma=False,
    )
```

```python
import jax
import jax.numpy as jnp
from jax import lax
from jax.experimental import pallas as pl
from jax.experimental.pallas import tpu as pltpu
from jax.sharding import PartitionSpec as P

AXES = ("gx", "gy")
TILES = 128
SLOTS = 112
ROWS = 256
LANES = 128
BANDS = ROWS // 8
HALO = 16
SUBS = 8
FIELDS = 8
FINAL = 5
I14 = 1.0 / 1.4
F32 = jnp.float32
VMEM_BYTES = 24 * 1024 * 1024


def specs(count):
    return [pl.BlockSpec(memory_space=pltpu.SMEM)] + [pl.BlockSpec(memory_space=pltpu.VMEM)] * (count - 1)


def lane_ids(rows=8):
    return lax.broadcasted_iota(jnp.int32, (rows, LANES), 1)


def roll(x, shift):
    return pltpu.roll(x, shift % LANES, 1) if shift % LANES else x


def interleave(tasks, width):
    tasks = list(tasks)
    active = []
    while tasks or active:
        if tasks and len(active) < width:
            active.append(tasks.pop(0))
        running = []
        for task in active:
            try:
                next(task)
                running.append(task)
            except StopIteration:
                pass
        active = running


def swap_chunks(quads, room):
    chunk = lane_ids() // 32
    moved = [[roll(x, 32 * c) for c, x in enumerate(quad)] for quad in quads]
    yield
    for q, quad in enumerate(moved):
        for c, x in enumerate(quad):
            room[q, c] = x
    yield
    out = []
    for q in range(len(quads)):
        kept = [room[q, c] for c in range(4)]
        rows = []
        for r in range(4):
            x = kept[-r % 4]
            for to in range(1, 4):
                x = jnp.where(chunk == to, kept[(to - r) % 4], x)
            rows.append(roll(x, -32 * r))
        out.append(rows)
    yield
    return out


def pack_kernel(*refs):
    far, refs = refs[:11], refs[11:]
    (out_ref, starts_ref, pos_ref, west_ref, east_ref), refs = refs[:5], refs[5:]
    here, (blk, starts_v, pos_v, scalars, sems) = refs[:11], refs[11:]
    ou_ref, ov_ref, wx_ref, wy_ref, _, owner_ref, con_ref, thk_ref, str_ref, mask_ref, vel_ref = here
    loads = [pltpu.make_async_copy(x, y, sems.at[n]) for n, (x, y) in enumerate(zip(far, here))]
    for n in (5, 0, 1, 2, 3, 6, 7, 8, 9, 10, 4):
        loads[n].start()
    loads[5].wait()
    me = lax.axis_index("gx") * lax.axis_size("gy") + lax.axis_index("gy")
    first = lax.broadcasted_iota(jnp.int32, (TILES, TILES), 0)
    second = lax.broadcasted_iota(jnp.int32, (TILES, TILES), 1)
    before = jnp.where(first < second, 1.0, 0.0)
    ones = jnp.ones((8, TILES), F32)
    owned = jnp.where(owner_ref[...] == me, 1.0, 0.0)
    counts = lax.dot_general(ones, owned, (((1,), (1,)), ((), ())), preferred_element_type=F32)
    starts = jnp.dot(counts, before, preferred_element_type=F32)
    starts_v[...] = starts.astype(jnp.int32)
    starts_copy = pltpu.make_async_copy(starts_v, starts_ref, scalars.at[0])
    starts_copy.start()

    mine = jnp.broadcast_to(owner_ref[pl.ds(me, 1), :], (TILES, TILES)).astype(F32)
    column = mine.T
    rank = jnp.dot(ones, jnp.where(column == mine, before, 0.0), preferred_element_type=F32)
    per_owner = jnp.dot(ones, jnp.where(column == second.astype(F32), 1.0, 0.0), preferred_element_type=F32)
    lane = lane_ids().astype(F32)
    free = jnp.min(jnp.where(per_owner < 2.0, lane, 1000.0), axis=1, keepdims=True)
    mine = mine[:8]
    icy = mine < TILES
    slot = jnp.where(icy, 2.0 * mine + rank, 2.0 * free + 1.0)
    row = lax.broadcasted_iota(jnp.int32, (8, TILES), 0)
    pos_v[...] = jnp.where(row == 0, slot, jnp.where(icy, 1.0, 0.0)).astype(jnp.int32)
    pos_copy = pltpu.make_async_copy(pos_v, pos_ref, scalars.at[1])
    pos_copy.start()

    for n in range(4):
        loads[n].wait()
    chunk = lane_ids() // HALO

    def sea_edges(i):
        moved = []
        for half in range(2):
            rows = slice(8 * i + half * LANES, 8 * i + half * LANES + 8)
            for f, ref in enumerate((ou_ref, ov_ref, wx_ref, wy_ref)):
                moved.append(roll(ref[rows, :], (4 * half + f) * HALO))
        yield
        west, east = moved[0], moved[0]
        for n in range(1, 8):
            west = jnp.where(chunk == n, moved[n], west)
            east = jnp.where(chunk == n - 1, moved[n], east)
        west_ref[8 * i : 8 * i + 8, :] = west
        east = roll(east, 2 * HALO)
        yield
        east_ref[8 * i : 8 * i + 8, :] = east

    interleave([sea_edges(i) for i in range(BANDS // 2)], 5)

    for n in range(6, 11):
        loads[n].wait()
    for g in range(SLOTS // 8):
        eight = slice(8 * g, 8 * g + 8)
        for h in range(2):
            cut = slice(h * LANES, (h + 1) * LANES)
            con = [con_ref[c, eight, cut] for c in range(5)]
            mass = sum(thk_ref[c, eight, cut] * con[c] for c in range(5))
            strength = mass * jnp.exp(-20.0 * (1.0 - sum(con)))
            rows = [str_ref[f, eight, cut] for f in range(3)]
            rows += [strength, mass, mask_ref[eight, cut].astype(F32)]
            for f, x in enumerate(rows):
                blk[pl.ds(128 * g + 8 * h + 2 + f, 8, stride=16), :] = x
            for j in range(8):
                at = 128 * g + 16 * j + 8 * h
                blk[at : at + 2, :] = vel_ref[8 * g + j, :, cut]

    loads[4].wait()
    starts_copy.wait()
    pos_copy.wait()
    for t in range(TILES):
        at = pl.multiple_of(starts_ref[0, t] * 16, 16)
        out_ref[2 * t] = blk[pl.ds(at, 16), :]
        out_ref[2 * t + 1] = blk[pl.ds(at + 16, 16), :]


def pack(owner_list, ice_mask, velocity, stress, thickness, concentration, maps):
    def by_field(x):
        return jnp.transpose(x, (1, 0, 2))

    inputs = (
        *maps, owner_list, by_field(concentration), by_field(thickness), by_field(stress), ice_mask, velocity
    )
    return pl.pallas_call(
        pack_kernel,
        in_specs=[pl.BlockSpec(memory_space=pltpu.HBM)] * 11,
        out_specs=[pl.BlockSpec(memory_space=pltpu.SMEM if n in (1, 2) else pltpu.VMEM) for n in range(10)],
        out_shape=(
            jax.ShapeDtypeStruct((2 * TILES, 2 * FIELDS, LANES), F32),
            pltpu.SMEM((8, TILES), jnp.int32),
            pltpu.SMEM((8, TILES), jnp.int32),
            jax.ShapeDtypeStruct((ROWS // 2, LANES), F32),
            jax.ShapeDtypeStruct((ROWS // 2, LANES), F32),
        )
        + (jax.ShapeDtypeStruct((ROWS, LANES), F32),) * 5,
        scratch_shapes=[pltpu.VMEM(x.shape, x.dtype) for x in inputs[5:]]
        + [
            pltpu.VMEM(((SLOTS + 8) * 16, LANES), F32),
            pltpu.VMEM((8, TILES), jnp.int32),
            pltpu.VMEM((8, TILES), jnp.int32),
            pltpu.SemaphoreType.DMA((2,)),
            pltpu.SemaphoreType.DMA((11,)),
        ],
        compiler_params=pltpu.CompilerParams(vmem_limit_bytes=VMEM_BYTES),
        name="pack",
    )(*(pltpu.with_memory_space_constraint(x, pltpu.HBM) for x in inputs))


def by_parity(axis, up, down):
    even = lax.axis_index(axis) % 2 == 0
    return jnp.where(even, up, down), jnp.where(even, down, up)


def unpack_tile_kernel(pos_ref, recv_ref, temp_ref, sea_west_ref, sea_east_ref, tile_ref, near_ref, far_ref, even_ref, room, edges):
    even_ref[...] = by_parity("gy", jnp.ones((8, LANES), F32), jnp.zeros((8, LANES), F32))[0]
    chunk = lane_ids() // HALO

    def band(i):
        base = i * 64
        rows = slice(8 * i, 8 * i + 8)
        quads = []
        for h in range(2):
            four = []
            for k in range(4 * i, 4 * i + 4):
                got = recv_ref[pos_ref[0, k], h * FIELDS : (h + 1) * FIELDS, :]
                four.append(jnp.where(pos_ref[1, k] > 0, got, 0.0))
            quads.append(four)
        quads = yield from swap_chunks(quads, room.at[i])
        for h in range(2):
            for r, x in enumerate(quads[h]):
                tile_ref[pl.ds(base + h * 4 + r, FIELDS, stride=8), :] = x
        melt = jnp.exp(-0.5 * jnp.maximum(temp_ref[rows, :], 0.0))
        yield
        moved = []
        for f in range(FIELDS):
            at = slice(base + 8 * f, base + 8 * f + 8)
            x = tile_ref[at, :]
            if f == 5:
                x = x * melt
                tile_ref[at, :] = x
            moved.append(roll(x, f * HALO))
        yield
        west, east = moved[0], moved[0]
        for f in range(1, FIELDS):
            west = jnp.where(chunk == f, moved[f], west)
            east = jnp.where(chunk == f - 1, moved[f], east)
        edges[0, rows, :] = west
        edges[1, rows, :] = east

    def edge(i):
        rows = slice(8 * i, 8 * i + 8)
        east = roll(edges[1, rows, :], 2 * HALO)
        yield
        near_ref[rows, :], far_ref[rows, :] = by_parity("gx", east, edges[0, rows, :])

    interleave([band(i) for i in range(BANDS)], 12)
    interleave([edge(i) for i in range(BANDS)], 16)
    near_ref[ROWS:, :], far_ref[ROWS:, :] = by_parity("gx", sea_east_ref[...], sea_west_ref[...])


EDGE = ROWS + ROWS // 2


def unpack_tile(pos, recv, temp, sea_west, sea_east):
    return pl.pallas_call(
        unpack_tile_kernel,
        in_specs=specs(5),
        out_shape=(
            jax.ShapeDtypeStruct((BANDS * FIELDS * 8, LANES), F32),
            jax.ShapeDtypeStruct((EDGE, LANES), F32),
            jax.ShapeDtypeStruct((EDGE, LANES), F32),
            jax.ShapeDtypeStruct((8, LANES), F32),
        ),
        scratch_shapes=[pltpu.VMEM((BANDS, 2, 4, 8, LANES), F32), pltpu.VMEM((2, ROWS, LANES), F32)],
        compiler_params=pltpu.CompilerParams(vmem_limit_bytes=VMEM_BYTES),
        name="unpack_tile",
    )(pos, recv, temp, sea_west, sea_east)


STATE = ("u", "v", "p", "m", "t")
STATIC = ("ou", "ov", "wx", "wy", "inertia", "turn", "k", "cover")


def put_ice(s, i, ice, row_ids, grid_rows):
    u, v, total, diff, shear, strength, mass, cover = ice
    at = slice(8 + 8 * i, 16 + 8 * i)
    here = slice(8 * i, 8 * i + 8)
    s["u"][at, :] = u
    s["v"][at, :] = v
    s["p"][at, :] = (0.25 * cover) * (total + diff)
    s["m"][at, :] = (0.25 * cover) * (total - diff)
    s["t"][at, :] = (0.5 * cover) * shear
    coriolis = 2.0 * (row_ids.astype(F32) + 0.5) / grid_rows - 1.0
    s["inertia"][here, :] = 2.0 * mass
    s["turn"][here, :] = mass * coriolis
    s["k"][here, :] = (0.1 * I14) * (cover * strength)
    s["cover"][here, :] = cover


def put_ocean(s, i, ocean):
    here = slice(8 * i, 8 * i + 8)
    for name, x in zip(("ou", "ov", "wx", "wy"), ocean):
        s[name][here, :] = x


def clear_ends(s, chunks):
    zero = jnp.zeros((8, LANES), F32)
    for name in STATE:
        s[name][0:8, :] = zero
        s[name][8 + 8 * chunks : 16 + 8 * chunks, :] = zero


def run_subcycles(s, stress_chunks, velocity_chunks, times=1):
    def subcycle(step, carry):
        for i in stress_chunks:
            a = 8 + 8 * i
            at, up, down = slice(a, a + 8), slice(a + 1, a + 9), slice(a - 1, a + 7)
            here = slice(8 * i, 8 * i + 8)
            u, v = s["u"][at, :], s["v"][at, :]
            exx = roll(u, -1) - roll(u, 1)
            eyy = s["v"][up, :] - s["v"][down, :]
            shear = (s["u"][up, :] - s["u"][down, :]) + (roll(v, -1) - roll(v, 1))
            div = exx + eyy
            ten = exx - eyy
            ten4, shear4 = 0.25 * ten, 0.25 * shear
            q = div * div + (ten * ten4 + shear * shear4) + 0.04
            inv = lax.rsqrt(q)
            k = s["k"][here, :] * inv
            base = div - q * inv
            s["p"][at, :] = I14 * s["p"][at, :] + k * (base + ten4)
            s["m"][at, :] = I14 * s["m"][at, :] + k * (base - ten4)
            s["t"][at, :] = I14 * s["t"][at, :] + k * shear4
        for i in velocity_chunks:
            a = 8 + 8 * i
            at, up, down = slice(a, a + 8), slice(a + 1, a + 9), slice(a - 1, a + 7)
            here = slice(8 * i, 8 * i + 8)
            p, t = s["p"][at, :], s["t"][at, :]
            fx = (roll(p, -1) - roll(p, 1)) + (s["t"][up, :] - s["t"][down, :])
            fy = (roll(t, -1) - roll(t, 1)) + (s["m"][up, :] - s["m"][down, :])
            u, v = s["u"][at, :], s["v"][at, :]
            ou, ov = s["ou"][here, :], s["ov"][here, :]
            du, dv = ou - u, ov - v
            g = du * du + dv * dv + 0.01
            drag = g * lax.rsqrt(g)
            inertia, turn = s["inertia"][here, :], s["turn"][here, :]
            diag = inertia + drag
            rx = inertia * u + fx + s["wx"][here, :] + drag * ou
            ry = inertia * v + fy + s["wy"][here, :] + drag * ov
            w = s["cover"][here, :] / (diag * diag + turn * turn)
            s["u"][at, :] = w * (diag * rx + turn * ry)
            s["v"][at, :] = w * (diag * ry - turn * rx)
        return carry

    if times == 1:
        subcycle(0, 0)
    else:
        lax.fori_loop(0, times // 4, lambda n, c: [subcycle(n, c) for _ in range(4)][-1], 0)


def state_scratch(chunks):
    tall = pltpu.VMEM((8 * chunks + 16, LANES), F32)
    flat = pltpu.VMEM((8 * chunks, LANES), F32)
    return [tall] * len(STATE) + [flat] * len(STATIC)


def named(scratch):
    return dict(zip(STATE + STATIC, scratch))


def at_row(i):
    return lax.axis_index("gy") * ROWS + 8 * i + lax.broadcasted_iota(jnp.int32, (8, LANES), 0)


def chunk_of(tile_ref, i):
    return [tile_ref[i * 64 + f * 8 : i * 64 + f * 8 + 8, :] for f in range(FIELDS)]


def stresses(p, m, t):
    return 2.0 * (p + m), 2.0 * (p - m), 2.0 * t


def state_of(s, i):
    at = slice(8 + 8 * i, 16 + 8 * i)
    return [s[name][at, :] for name in STATE]


def inner_kernel(tile_ref, ou_ref, ov_ref, wx_ref, wy_ref, out_ref, *scratch):
    s = named(scratch)
    grid_rows = ROWS * lax.axis_size("gy")
    clear_ends(s, BANDS)
    for i in range(BANDS):
        put_ice(s, i, chunk_of(tile_ref, i), at_row(i), grid_rows)
        put_ocean(s, i, [ref[8 * i : 8 * i + 8, :] for ref in (ou_ref, ov_ref, wx_ref, wy_ref)])
    run_subcycles(s, range(BANDS), range(BANDS), SUBS)
    for i in range(BANDS):
        for f, x in enumerate(state_of(s, i)):
            out_ref[f, 8 * i : 8 * i + 8, :] = x


def inner(tile, ocean):
    return pl.pallas_call(
        inner_kernel,
        out_shape=jax.ShapeDtypeStruct((FINAL, ROWS, LANES), F32),
        scratch_shapes=state_scratch(BANDS),
        compiler_params=pltpu.CompilerParams(vmem_limit_bytes=VMEM_BYTES),
        cost_estimate=pl.CostEstimate(flops=4_000_000, bytes_accessed=4_000_000, transcendentals=800_000),
        name="inner",
    )(tile, *ocean)


def strip_moves(own, west, east, n, lane):
    halo = jnp.where(lane // HALO == n, east, west)
    return own, roll(own, -32), roll(halo, (6 - n) * HALO)


def strip(own, moved, halo, lane):
    return jnp.where(lane >= 96, halo, jnp.where(lane < 48, own, moved))


def ice_strips(own, west, east, edge, lane):
    west = jnp.where(edge[0], 0.0, west)
    east = jnp.where(edge[1], 0.0, east)
    moved = [strip_moves(own[f], west, east, f, lane) for f in range(FIELDS)]
    yield
    return [strip(*x, lane) for x in moved]


def ocean_strips(own, west, east, half, lane):
    moved = [strip_moves(own[f], west, east, 4 * half + f, lane) for f in range(4)]
    yield
    return [strip(*x, lane) for x in moved]


def edges_x():
    a = lax.axis_index("gx")
    return a == 0, a == lax.axis_size("gx") - 1


def edges_y():
    b = lax.axis_index("gy")
    return b == 0, b == lax.axis_size("gy") - 1


def join(mid, strips, moved, lane):
    x = jnp.where(lane < HALO, strips, mid)
    return jnp.where(lane >= LANES - HALO, moved, x)


def finish_band(band, mids, strips, refs, drag_ref, stage, room, lane):
    pos_ref, tile_ref, ou_ref, ov_ref, packed_ref = refs
    moved = [roll(x, 32) for x in strips()]
    yield
    u, v, *pmt = [join(*x, lane) for x in zip(mids(), strips(), moved)]
    five = [u, v, *stresses(*pmt)]
    for f, x in enumerate(five):
        for h in range(2):
            at = h * 32 + f * 4
            stage[at : at + 4, :] = x[4 * h : 4 * h + 4, :]
    rows = slice(8 * band, 8 * band + 8)
    cover = tile_ref[band * 64 + 56 : band * 64 + 64, :]
    drag_ref[0], drag_ref[1] = drag_rows(five, ou_ref[rows, :], ov_ref[rows, :], cover)
    yield
    quads = [[stage[pl.ds(32 * h + r, 8, stride=4), :] for r in range(4)] for h in range(2)]
    quads = yield from swap_chunks(quads, room)
    for c in range(4):
        at = pos_ref[0, band * 4 + c] * 2 * FINAL
        for h in range(2):
            packed_ref[pl.ds(at + h * FINAL, FINAL), :] = quads[h][c][:FINAL]


def drag_rows(five, ou, ov, cover):
    du, dv = five[0] - ou, five[1] - ov
    g = du * du + dv * dv + 0.01
    drag = cover * (g * lax.rsqrt(g))
    return drag * du, drag * dv


def sides_kernel(
    pos_ref, tile_ref, near_ref, far_ref, ou_ref, ov_ref, wx_ref, wy_ref, mid_ref, packed_ref, drag_ref, stage, room, *scratch,
):
    s = named(scratch)
    lane = lane_ids()
    grid_rows = ROWS * lax.axis_size("gy")
    edge = edges_x()
    clear_ends(s, BANDS)

    def start(i):
        rows = slice(8 * i, 8 * i + 8)
        east, west = by_parity("gx", near_ref[rows, :], far_ref[rows, :])
        ice = yield from ice_strips(chunk_of(tile_ref, i), west, east, edge, lane)
        put_ice(s, i, ice, at_row(i), grid_rows)
        half, j = divmod(i, BANDS // 2)
        sea = slice(ROWS + 8 * j, ROWS + 8 * j + 8)
        own = [ref[rows, :] for ref in (ou_ref, ov_ref, wx_ref, wy_ref)]
        east, west = by_parity("gx", near_ref[sea, :], far_ref[sea, :])
        put_ocean(s, i, (yield from ocean_strips(own, west, east, half, lane)))

    interleave([start(i) for i in range(BANDS)], 3)
    run_subcycles(s, range(BANDS), range(BANDS), SUBS)
    refs = (pos_ref, tile_ref, ou_ref, ov_ref, packed_ref)

    def finish(i):
        def mids():
            return [mid_ref[f, 8 * i : 8 * i + 8, :] for f in range(FINAL)]

        drag = drag_ref.at[:, pl.ds(8 * i - HALO, 8), :]
        yield from finish_band(i, mids, lambda: state_of(s, i), refs, drag, stage.at[i], room.at[i], lane)

    interleave([finish(i) for i in range(2, BANDS - 2)], 8)


def stage_scratch(bands):
    return [pltpu.VMEM((bands, 64, LANES), F32), pltpu.VMEM((bands, 2, 4, 8, LANES), F32)]


def results(rows):
    return pltpu.VMEM((2 * TILES * 2 * FINAL, LANES), F32), jax.ShapeDtypeStruct((2, rows, LANES), F32)


def sides(pos, tile, west, east, ocean, mid):
    return pl.pallas_call(
        sides_kernel,
        in_specs=specs(9),
        out_shape=results(ROWS - 2 * HALO),
        out_specs=specs(3)[1:],
        scratch_shapes=stage_scratch(BANDS) + state_scratch(BANDS),
        compiler_params=pltpu.CompilerParams(vmem_limit_bytes=VMEM_BYTES),
        cost_estimate=pl.CostEstimate(flops=5_000_000, bytes_accessed=5_000_000, transcendentals=800_000),
        name="sides",
    )(pos, tile, west, east, *ocean, mid)


def ends_kernel(
    pos_ref, tile_ref, near_ref, far_ref, inner_ref, outer_ref, ou_ref, ov_ref, wx_ref, wy_ref,
    packed_in, packed_ref, drag_ref, stage, room, *scratch,
):
    del packed_in
    s = named(scratch)
    lane = lane_ids()
    grid_rows = ROWS * lax.axis_size("gy")
    edge = edges_x()
    outside = edges_y()
    ocean_refs = (ou_ref, ov_ref, wx_ref, wy_ref)
    clear_ends(s, 24)

    def start(end, j):
        i = (j - 2) if end == 0 else BANDS - 4 + j
        half = 1 - end if not 0 <= i < BANDS else i // (BANDS // 2)
        if 0 <= i < BANDS:
            rows = slice(8 * i, 8 * i + 8)
            own = chunk_of(tile_ref, i)
            east, west = by_parity("gx", near_ref[rows, :], far_ref[rows, :])
            water = [x[rows, :] for x in ocean_refs]
            at = ROWS + 8 * (i % (BANDS // 2))
            sea_east, sea_west = by_parity("gx", near_ref[at : at + 8, :], far_ref[at : at + 8, :])
        else:
            at = 8 * (i % 2)

            def part_of(base):
                rows = slice(base, base + 8)
                south, north = by_parity("gy", inner_ref[rows, :], outer_ref[rows, :])
                return south if end else north

            own = [jnp.where(outside[end], 0.0, part_of(i % 2 * 64 + 8 * f)) for f in range(FIELDS)]
            east, west = by_parity("gx", part_of(128 + at), part_of(144 + at))
            west, east = jnp.where(outside[end], 0.0, west), jnp.where(outside[end], 0.0, east)
            water = [part_of(160 + 16 * f + at) for f in range(4)]
            sea_east, sea_west = by_parity("gx", part_of(224 + at), part_of(240 + at))
        for part in range(2):
            chunk = part * 12 + end * 6 + j
            ice = (yield from ice_strips(own, west, east, edge, lane)) if part else own
            put_ice(s, chunk, ice, at_row(i), grid_rows)
            if part:
                water = yield from ocean_strips(water, sea_west, sea_east, half, lane)
            put_ocean(s, chunk, water)

    interleave([start(end, j) for end in range(2) for j in range(6)], 3)
    every = range(24)
    four = [c for c in every if c % 6 not in (0, 5)]
    two = [c for c in every if c % 6 in (2, 3)]
    for step in range(1, SUBS + 1):
        stress = every if step < 5 else four
        run_subcycles(s, stress, every if step < 4 else four if step < 8 else two)
    refs = (pos_ref, tile_ref, ou_ref, ov_ref, packed_ref)

    def finish(n):
        end, j = divmod(n, 2)
        chunk = end * 6 + j + 2
        i = BANDS - 2 + j if end else j
        drag = drag_ref.at[:, pl.ds(8 * n, 8), :]
        yield from finish_band(i, lambda: state_of(s, chunk), lambda: state_of(s, chunk + 12), refs, drag, stage.at[n], room.at[n], lane)

    interleave([finish(n) for n in range(4)], 4)


def ends(pos, tile, west, east, north, south, ocean, packed):
    packed = pltpu.with_memory_space_constraint(packed, pltpu.VMEM)
    return pl.pallas_call(
        ends_kernel,
        in_specs=specs(11),
        out_shape=results(2 * HALO),
        out_specs=specs(3)[1:],
        input_output_aliases={10: 0},
        scratch_shapes=stage_scratch(4) + state_scratch(24),
        compiler_params=pltpu.CompilerParams(vmem_limit_bytes=VMEM_BYTES),
        name="ends",
    )(pos, tile, west, east, north, south, *ocean, packed)


def unpack_ice_kernel(starts_ref, recv_ref, mid_ref, end_ref, vel_out, str_out, drag_out, blk, vel_ref, str_ref, sems):
    first, last = pl.ds(0, HALO), pl.ds(ROWS - HALO, HALO)
    copies = [
        pltpu.make_async_copy(mid_ref, drag_out.at[:, pl.ds(HALO, ROWS - 2 * HALO), :], sems.at[0]),
        pltpu.make_async_copy(end_ref.at[:, first, :], drag_out.at[:, first, :], sems.at[1]),
        pltpu.make_async_copy(end_ref.at[:, pl.ds(HALO, HALO), :], drag_out.at[:, last, :], sems.at[2]),
    ]
    for copy in copies:
        copy.start()
    for t in range(TILES):
        start = starts_ref[0, t]
        for c in range(2):
            at = (2 * t + c) * 2 * FINAL
            to = pl.multiple_of((start + c) * 16, 16)
            blk[pl.ds(to, 2 * FINAL), :] = recv_ref[at : at + 2 * FINAL, :]
    half = SLOTS // 2
    for part in range(2):
        for g in range(part * half // 8, (part + 1) * half // 8):
            eight = slice(8 * g, 8 * g + 8)
            for h in range(2):
                cut = slice(h * LANES, (h + 1) * LANES)
                for f in range(3):
                    str_ref[f, eight, cut] = blk[pl.ds(128 * g + h * FINAL + 2 + f, 8, stride=16), :]
                for j in range(8):
                    at = 128 * g + 16 * j + h * FINAL
                    vel_ref[8 * g + j, :, cut] = blk[at : at + 2, :]
        some = pl.ds(part * half, half)
        parts = [
            pltpu.make_async_copy(vel_ref.at[some], vel_out.at[some], sems.at[3 + 2 * part]),
            pltpu.make_async_copy(str_ref.at[:, some, :], str_out.at[:, some, :], sems.at[4 + 2 * part]),
        ]
        for copy in parts:
            copy.start()
        copies += parts
    for copy in copies:
        copy.wait()


def unpack_ice(starts, recv, drag_mid, drag_ends):
    vel_shape, str_shape = (SLOTS, 2, 2 * LANES), (3, SLOTS, 2 * LANES)
    vel, strs, drag = pl.pallas_call(
        unpack_ice_kernel,
        in_specs=specs(4),
        out_specs=[pl.BlockSpec(memory_space=pltpu.HBM)] * 3,
        out_shape=tuple(pltpu.HBM(shape, F32) for shape in (vel_shape, str_shape, (2, ROWS, LANES))),
        scratch_shapes=[
            pltpu.VMEM(((SLOTS + 8) * 16, LANES), F32),
            pltpu.VMEM(vel_shape, F32),
            pltpu.VMEM(str_shape, F32),
            pltpu.SemaphoreType.DMA((7,)),
        ],
        compiler_params=pltpu.CompilerParams(vmem_limit_bytes=VMEM_BYTES),
        name="unpack_ice",
    )(starts, recv, drag_mid, drag_ends)
    return vel, jnp.transpose(strs, (1, 0, 2)), drag


def exchange(axis, near, far):
    nx, ny = lax.axis_size("gx"), lax.axis_size("gy")
    swaps = ([], [])
    for a in range(nx):
        for b in range(ny):
            at, n = (a, nx) if axis == "gx" else (b, ny)
            for swap, step in zip(swaps, (1 - at % 2 * 2, at % 2 * 2 - 1)):
                to = (a + step, b) if axis == "gx" else (a, b + step)
                if not 0 <= at + step < n:
                    to = (a, b ^ 1) if axis == "gx" else (a ^ 1, b)
                swap.append((a * ny + b, to[0] * ny + to[1]))
    far = lax.ppermute(far, AXES, swaps[1])
    return lax.ppermute(near, AXES, swaps[0]), far


def on_device(
    owner_list, ice_mask, velocity, stress, thickness, concentration, ocean_u, ocean_v, wind_x, wind_y, surface_temp
):
    ocean = (ocean_u, ocean_v, wind_x, wind_y)
    outbound, starts, pos, sea_west, sea_east, *maps = pack(
        owner_list, ice_mask, velocity, stress, thickness, concentration, (*ocean, surface_temp)
    )
    *ocean, surface_temp = maps
    arrived = lax.all_to_all(outbound, AXES, split_axis=0, concat_axis=0, tiled=True)
    tile, near, far, even = unpack_tile(pos, arrived, surface_temp, sea_west, sea_east)
    near, far = exchange("gx", near, far)
    near, far, mid, *ocean = lax.optimization_barrier((near, far, inner(tile, ocean), *ocean))

    def edge(cells, block_rows, sea_rows):
        parts = [tile[block_rows], near[:ROWS][cells], far[:ROWS][cells]]
        parts += [x[cells] for x in ocean] + [near[sea_rows], far[sea_rows]]
        return jnp.concatenate(parts, axis=0)

    low = edge(slice(0, HALO), slice(0, 128), slice(ROWS, ROWS + HALO))
    high = edge(slice(ROWS - HALO, ROWS), slice(-128, None), slice(EDGE - HALO, EDGE))
    even = even[:1] > 0.5
    near_y, far_y = exchange("gy", jnp.where(even, high, low), jnp.where(even, low, high))
    packed, drag_mid = sides(pos, tile, near, far, ocean, mid)
    packed, drag_ends = ends(pos, tile, near, far, near_y, far_y, ocean, packed)

    homeward = packed.reshape(2 * TILES, FINAL, 2, LANES)
    back = lax.all_to_all(homeward, AXES, split_axis=0, concat_axis=0, tiled=True)
    return unpack_ice(starts, back.reshape(2 * TILES * 2 * FINAL, LANES), drag_mid, drag_ends)


def solution(mesh):
    blocks = P(AXES, None, None)
    return jax.shard_map(
        on_device,
        mesh=mesh,
        in_specs=(P(), P(AXES, None)) + (blocks,) * 4 + (P("gy", "gx"),) * 5,
        out_specs=(blocks, blocks, P(None, "gy", "gx")),
        check_vma=False,
    )
```

```python
import jax
import jax.numpy as jnp
from jax import lax
from jax.experimental import pallas as pl
from jax.experimental.pallas import tpu as pltpu
from jax.sharding import PartitionSpec as P

AXES = ("gx", "gy")
TILES = 128
SLOTS = 112
ROWS = 256
LANES = 128
BANDS = ROWS // 8
HALO = 16
SUBS = 8
FIELDS = 8
FINAL = 5
I14 = 1.0 / 1.4
F32 = jnp.float32
VMEM_BYTES = 24 * 1024 * 1024


def specs(count):
    return [pl.BlockSpec(memory_space=pltpu.SMEM)] + [pl.BlockSpec(memory_space=pltpu.VMEM)] * (count - 1)


def lane_ids(rows=8):
    return lax.broadcasted_iota(jnp.int32, (rows, LANES), 1)


def roll(x, shift):
    return pltpu.roll(x, shift % LANES, 1) if shift % LANES else x


def interleave(tasks, width):
    tasks = list(tasks)
    active = []
    while tasks or active:
        if tasks and len(active) < width:
            active.append(tasks.pop(0))
        running = []
        for task in active:
            try:
                next(task)
                running.append(task)
            except StopIteration:
                pass
        active = running


def swap_chunks(quads, room):
    chunk = lane_ids() // 32
    moved = [[roll(x, 32 * c) for c, x in enumerate(quad)] for quad in quads]
    yield
    for q, quad in enumerate(moved):
        for c, x in enumerate(quad):
            room[q, c] = x
    yield
    out = []
    for q in range(len(quads)):
        kept = [room[q, c] for c in range(4)]
        rows = []
        for r in range(4):
            x = kept[-r % 4]
            for to in range(1, 4):
                x = jnp.where(chunk == to, kept[(to - r) % 4], x)
            rows.append(roll(x, -32 * r))
        out.append(rows)
    yield
    return out


def pack_kernel(*refs):
    far, refs = refs[:11], refs[11:]
    (out_ref, starts_ref, pos_ref, west_ref, east_ref), refs = refs[:5], refs[5:]
    here, (blk, starts_v, pos_v, scalars, sems) = refs[:11], refs[11:]
    ou_ref, ov_ref, wx_ref, wy_ref, _, owner_ref, con_ref, thk_ref, str_ref, mask_ref, vel_ref = here
    loads = [pltpu.make_async_copy(x, y, sems.at[n]) for n, (x, y) in enumerate(zip(far, here))]
    for n in (5, 6, 7, 8, 9, 10, 0, 1, 2, 3, 4):
        loads[n].start()
    loads[5].wait()
    me = lax.axis_index("gx") * lax.axis_size("gy") + lax.axis_index("gy")
    first = lax.broadcasted_iota(jnp.int32, (TILES, TILES), 0)
    second = lax.broadcasted_iota(jnp.int32, (TILES, TILES), 1)
    before = jnp.where(first < second, 1.0, 0.0)
    ones = jnp.ones((8, TILES), F32)
    owned = jnp.where(owner_ref[...] == me, 1.0, 0.0)
    counts = lax.dot_general(ones, owned, (((1,), (1,)), ((), ())), preferred_element_type=F32)
    starts = jnp.dot(counts, before, preferred_element_type=F32)
    starts_v[...] = starts.astype(jnp.int32)
    starts_copy = pltpu.make_async_copy(starts_v, starts_ref, scalars.at[0])
    starts_copy.start()

    mine = jnp.broadcast_to(owner_ref[pl.ds(me, 1), :], (TILES, TILES)).astype(F32)
    column = mine.T
    rank = jnp.dot(ones, jnp.where(column == mine, before, 0.0), preferred_element_type=F32)
    per_owner = jnp.dot(ones, jnp.where(column == second.astype(F32), 1.0, 0.0), preferred_element_type=F32)
    lane = lane_ids().astype(F32)
    free = jnp.min(jnp.where(per_owner < 2.0, lane, 1000.0), axis=1, keepdims=True)
    mine = mine[:8]
    icy = mine < TILES
    slot = jnp.where(icy, 2.0 * mine + rank, 2.0 * free + 1.0)
    row = lax.broadcasted_iota(jnp.int32, (8, TILES), 0)
    pos_v[...] = jnp.where(row == 0, slot, jnp.where(icy, 1.0, 0.0)).astype(jnp.int32)
    pos_copy = pltpu.make_async_copy(pos_v, pos_ref, scalars.at[1])
    pos_copy.start()

    for n in range(6, 11):
        loads[n].wait()
    for g in range(SLOTS // 8):
        eight = slice(8 * g, 8 * g + 8)
        for h in range(2):
            cut = slice(h * LANES, (h + 1) * LANES)
            con = [con_ref[c, eight, cut] for c in range(5)]
            mass = sum(thk_ref[c, eight, cut] * con[c] for c in range(5))
            strength = mass * jnp.exp(-20.0 * (1.0 - sum(con)))
            rows = [str_ref[f, eight, cut] for f in range(3)]
            rows += [strength, mass, mask_ref[eight, cut].astype(F32)]
            for f, x in enumerate(rows):
                blk[pl.ds(128 * g + 8 * h + 2 + f, 8, stride=16), :] = x
            for j in range(8):
                at = 128 * g + 16 * j + 8 * h
                blk[at : at + 2, :] = vel_ref[8 * g + j, :, cut]

    starts_copy.wait()
    for t in range(TILES):
        at = pl.multiple_of(starts_ref[0, t] * 16, 16)
        out_ref[2 * t] = blk[pl.ds(at, 16), :]
        out_ref[2 * t + 1] = blk[pl.ds(at + 16, 16), :]

    for n in range(4):
        loads[n].wait()
    chunk = lane_ids() // HALO

    def sea_edges(i):
        moved = []
        for half in range(2):
            rows = slice(8 * i + half * LANES, 8 * i + half * LANES + 8)
            for f, ref in enumerate((ou_ref, ov_ref, wx_ref, wy_ref)):
                moved.append(roll(ref[rows, :], (4 * half + f) * HALO))
        yield
        west, east = moved[0], moved[0]
        for n in range(1, 8):
            west = jnp.where(chunk == n, moved[n], west)
            east = jnp.where(chunk == n - 1, moved[n], east)
        west_ref[8 * i : 8 * i + 8, :] = west
        east = roll(east, 2 * HALO)
        yield
        east_ref[8 * i : 8 * i + 8, :] = east

    interleave([sea_edges(i) for i in range(BANDS // 2)], 5)
    loads[4].wait()
    pos_copy.wait()


def pack(owner_list, ice_mask, velocity, stress, thickness, concentration, maps):
    def by_field(x):
        return jnp.transpose(x, (1, 0, 2))

    inputs = (
        *maps, owner_list, by_field(concentration), by_field(thickness), by_field(stress), ice_mask, velocity
    )
    return pl.pallas_call(
        pack_kernel,
        in_specs=[pl.BlockSpec(memory_space=pltpu.HBM)] * 11,
        out_specs=[pl.BlockSpec(memory_space=pltpu.SMEM if n in (1, 2) else pltpu.VMEM) for n in range(10)],
        out_shape=(
            jax.ShapeDtypeStruct((2 * TILES, 2 * FIELDS, LANES), F32),
            pltpu.SMEM((8, TILES), jnp.int32),
            pltpu.SMEM((8, TILES), jnp.int32),
            jax.ShapeDtypeStruct((ROWS // 2, LANES), F32),
            jax.ShapeDtypeStruct((ROWS // 2, LANES), F32),
        )
        + (jax.ShapeDtypeStruct((ROWS, LANES), F32),) * 5,
        scratch_shapes=[pltpu.VMEM(x.shape, x.dtype) for x in inputs[5:]]
        + [
            pltpu.VMEM(((SLOTS + 8) * 16, LANES), F32),
            pltpu.VMEM((8, TILES), jnp.int32),
            pltpu.VMEM((8, TILES), jnp.int32),
            pltpu.SemaphoreType.DMA((2,)),
            pltpu.SemaphoreType.DMA((11,)),
        ],
        compiler_params=pltpu.CompilerParams(vmem_limit_bytes=VMEM_BYTES),
        name="pack",
    )(*(pltpu.with_memory_space_constraint(x, pltpu.HBM) for x in inputs))


def by_parity(axis, up, down):
    even = lax.axis_index(axis) % 2 == 0
    return jnp.where(even, up, down), jnp.where(even, down, up)


def unpack_tile_kernel(pos_ref, recv_ref, temp_ref, sea_west_ref, sea_east_ref, tile_ref, near_ref, far_ref, even_ref, room, edges):
    even_ref[...] = by_parity("gy", jnp.ones((8, LANES), F32), jnp.zeros((8, LANES), F32))[0]
    chunk = lane_ids() // HALO

    def band(i):
        base = i * 64
        rows = slice(8 * i, 8 * i + 8)
        quads = []
        for h in range(2):
            four = []
            for k in range(4 * i, 4 * i + 4):
                got = recv_ref[pos_ref[0, k], h * FIELDS : (h + 1) * FIELDS, :]
                four.append(jnp.where(pos_ref[1, k] > 0, got, 0.0))
            quads.append(four)
        quads = yield from swap_chunks(quads, room.at[i])
        for h in range(2):
            for r, x in enumerate(quads[h]):
                tile_ref[pl.ds(base + h * 4 + r, FIELDS, stride=8), :] = x
        melt = jnp.exp(-0.5 * jnp.maximum(temp_ref[rows, :], 0.0))
        yield
        moved = []
        for f in range(FIELDS):
            at = slice(base + 8 * f, base + 8 * f + 8)
            x = tile_ref[at, :]
            if f == 5:
                x = x * melt
                tile_ref[at, :] = x
            moved.append(roll(x, f * HALO))
        yield
        west, east = moved[0], moved[0]
        for f in range(1, FIELDS):
            west = jnp.where(chunk == f, moved[f], west)
            east = jnp.where(chunk == f - 1, moved[f], east)
        edges[0, rows, :] = west
        edges[1, rows, :] = east

    def edge(i):
        rows = slice(8 * i, 8 * i + 8)
        east = roll(edges[1, rows, :], 2 * HALO)
        yield
        near_ref[rows, :], far_ref[rows, :] = by_parity("gx", east, edges[0, rows, :])

    interleave([band(i) for i in range(BANDS)], 12)
    interleave([edge(i) for i in range(BANDS)], 16)
    near_ref[ROWS:, :], far_ref[ROWS:, :] = by_parity("gx", sea_east_ref[...], sea_west_ref[...])


EDGE = ROWS + ROWS // 2


def unpack_tile(pos, recv, temp, sea_west, sea_east):
    return pl.pallas_call(
        unpack_tile_kernel,
        in_specs=specs(5),
        out_shape=(
            jax.ShapeDtypeStruct((BANDS * FIELDS * 8, LANES), F32),
            jax.ShapeDtypeStruct((EDGE, LANES), F32),
            jax.ShapeDtypeStruct((EDGE, LANES), F32),
            jax.ShapeDtypeStruct((8, LANES), F32),
        ),
        scratch_shapes=[pltpu.VMEM((BANDS, 2, 4, 8, LANES), F32), pltpu.VMEM((2, ROWS, LANES), F32)],
        compiler_params=pltpu.CompilerParams(vmem_limit_bytes=VMEM_BYTES),
        name="unpack_tile",
    )(pos, recv, temp, sea_west, sea_east)


STATE = ("u", "v", "p", "m", "t")
STATIC = ("ou", "ov", "wx", "wy", "inertia", "turn", "k", "cover")


def put_ice(s, i, ice, row_ids, grid_rows):
    u, v, total, diff, shear, strength, mass, cover = ice
    at = slice(8 + 8 * i, 16 + 8 * i)
    here = slice(8 * i, 8 * i + 8)
    s["u"][at, :] = u
    s["v"][at, :] = v
    s["p"][at, :] = (0.25 * cover) * (total + diff)
    s["m"][at, :] = (0.25 * cover) * (total - diff)
    s["t"][at, :] = (0.5 * cover) * shear
    coriolis = 2.0 * (row_ids.astype(F32) + 0.5) / grid_rows - 1.0
    s["inertia"][here, :] = 2.0 * mass
    s["turn"][here, :] = mass * coriolis
    s["k"][here, :] = (0.1 * I14) * (cover * strength)
    s["cover"][here, :] = cover


def put_ocean(s, i, ocean):
    here = slice(8 * i, 8 * i + 8)
    for name, x in zip(("ou", "ov", "wx", "wy"), ocean):
        s[name][here, :] = x


def clear_ends(s, chunks):
    zero = jnp.zeros((8, LANES), F32)
    for name in STATE:
        s[name][0:8, :] = zero
        s[name][8 + 8 * chunks : 16 + 8 * chunks, :] = zero


def run_subcycles(s, stress_chunks, velocity_chunks, times=1):
    def subcycle(step, carry):
        for i in stress_chunks:
            a = 8 + 8 * i
            at, up, down = slice(a, a + 8), slice(a + 1, a + 9), slice(a - 1, a + 7)
            here = slice(8 * i, 8 * i + 8)
            u, v = s["u"][at, :], s["v"][at, :]
            exx = roll(u, -1) - roll(u, 1)
            eyy = s["v"][up, :] - s["v"][down, :]
            shear = (s["u"][up, :] - s["u"][down, :]) + (roll(v, -1) - roll(v, 1))
            div = exx + eyy
            ten = exx - eyy
            ten4, shear4 = 0.25 * ten, 0.25 * shear
            q = div * div + (ten * ten4 + shear * shear4) + 0.04
            inv = lax.rsqrt(q)
            k = s["k"][here, :] * inv
            base = div - q * inv
            s["p"][at, :] = I14 * s["p"][at, :] + k * (base + ten4)
            s["m"][at, :] = I14 * s["m"][at, :] + k * (base - ten4)
            s["t"][at, :] = I14 * s["t"][at, :] + k * shear4
        for i in velocity_chunks:
            a = 8 + 8 * i
            at, up, down = slice(a, a + 8), slice(a + 1, a + 9), slice(a - 1, a + 7)
            here = slice(8 * i, 8 * i + 8)
            p, t = s["p"][at, :], s["t"][at, :]
            fx = (roll(p, -1) - roll(p, 1)) + (s["t"][up, :] - s["t"][down, :])
            fy = (roll(t, -1) - roll(t, 1)) + (s["m"][up, :] - s["m"][down, :])
            u, v = s["u"][at, :], s["v"][at, :]
            ou, ov = s["ou"][here, :], s["ov"][here, :]
            du, dv = ou - u, ov - v
            g = du * du + dv * dv + 0.01
            drag = g * lax.rsqrt(g)
            inertia, turn = s["inertia"][here, :], s["turn"][here, :]
            diag = inertia + drag
            rx = inertia * u + fx + s["wx"][here, :] + drag * ou
            ry = inertia * v + fy + s["wy"][here, :] + drag * ov
            w = s["cover"][here, :] / (diag * diag + turn * turn)
            s["u"][at, :] = w * (diag * rx + turn * ry)
            s["v"][at, :] = w * (diag * ry - turn * rx)
        return carry

    if times == 1:
        subcycle(0, 0)
    else:
        lax.fori_loop(0, times // 4, lambda n, c: [subcycle(n, c) for _ in range(4)][-1], 0)


def state_scratch(chunks):
    tall = pltpu.VMEM((8 * chunks + 16, LANES), F32)
    flat = pltpu.VMEM((8 * chunks, LANES), F32)
    return [tall] * len(STATE) + [flat] * len(STATIC)


def named(scratch):
    return dict(zip(STATE + STATIC, scratch))


def at_row(i):
    return lax.axis_index("gy") * ROWS + 8 * i + lax.broadcasted_iota(jnp.int32, (8, LANES), 0)


def chunk_of(tile_ref, i):
    return [tile_ref[i * 64 + f * 8 : i * 64 + f * 8 + 8, :] for f in range(FIELDS)]


def stresses(p, m, t):
    return 2.0 * (p + m), 2.0 * (p - m), 2.0 * t


def state_of(s, i):
    at = slice(8 + 8 * i, 16 + 8 * i)
    return [s[name][at, :] for name in STATE]


def inner_kernel(tile_ref, ou_ref, ov_ref, wx_ref, wy_ref, out_ref, *scratch):
    s = named(scratch)
    grid_rows = ROWS * lax.axis_size("gy")
    clear_ends(s, BANDS)
    for i in range(BANDS):
        put_ice(s, i, chunk_of(tile_ref, i), at_row(i), grid_rows)
        put_ocean(s, i, [ref[8 * i : 8 * i + 8, :] for ref in (ou_ref, ov_ref, wx_ref, wy_ref)])
    run_subcycles(s, range(BANDS), range(BANDS), SUBS)
    for i in range(BANDS):
        for f, x in enumerate(state_of(s, i)):
            out_ref[f, 8 * i : 8 * i + 8, :] = x


def inner(tile, ocean):
    return pl.pallas_call(
        inner_kernel,
        out_shape=jax.ShapeDtypeStruct((FINAL, ROWS, LANES), F32),
        scratch_shapes=state_scratch(BANDS),
        compiler_params=pltpu.CompilerParams(vmem_limit_bytes=VMEM_BYTES),
        cost_estimate=pl.CostEstimate(flops=4_000_000, bytes_accessed=4_000_000, transcendentals=800_000),
        name="inner",
    )(tile, *ocean)


def strip_moves(own, west, east, n, lane):
    halo = jnp.where(lane // HALO == n, east, west)
    return own, roll(own, -32), roll(halo, (6 - n) * HALO)


def strip(own, moved, halo, lane):
    return jnp.where(lane >= 96, halo, jnp.where(lane < 48, own, moved))


def ice_strips(own, west, east, edge, lane):
    west = jnp.where(edge[0], 0.0, west)
    east = jnp.where(edge[1], 0.0, east)
    moved = [strip_moves(own[f], west, east, f, lane) for f in range(FIELDS)]
    yield
    return [strip(*x, lane) for x in moved]


def ocean_strips(own, west, east, half, lane):
    moved = [strip_moves(own[f], west, east, 4 * half + f, lane) for f in range(4)]
    yield
    return [strip(*x, lane) for x in moved]


def edges_x():
    a = lax.axis_index("gx")
    return a == 0, a == lax.axis_size("gx") - 1


def edges_y():
    b = lax.axis_index("gy")
    return b == 0, b == lax.axis_size("gy") - 1


def join(mid, strips, moved, lane):
    x = jnp.where(lane < HALO, strips, mid)
    return jnp.where(lane >= LANES - HALO, moved, x)


def finish_band(band, mids, strips, refs, drag_ref, stage, room, lane):
    pos_ref, tile_ref, ou_ref, ov_ref, packed_ref = refs
    moved = [roll(x, 32) for x in strips()]
    yield
    u, v, *pmt = [join(*x, lane) for x in zip(mids(), strips(), moved)]
    five = [u, v, *stresses(*pmt)]
    for f, x in enumerate(five):
        for h in range(2):
            at = h * 32 + f * 4
            stage[at : at + 4, :] = x[4 * h : 4 * h + 4, :]
    rows = slice(8 * band, 8 * band + 8)
    cover = tile_ref[band * 64 + 56 : band * 64 + 64, :]
    drag_ref[0], drag_ref[1] = drag_rows(five, ou_ref[rows, :], ov_ref[rows, :], cover)
    yield
    quads = [[stage[pl.ds(32 * h + r, 8, stride=4), :] for r in range(4)] for h in range(2)]
    quads = yield from swap_chunks(quads, room)
    for c in range(4):
        at = pos_ref[0, band * 4 + c] * 2 * FINAL
        for h in range(2):
            packed_ref[pl.ds(at + h * FINAL, FINAL), :] = quads[h][c][:FINAL]


def drag_rows(five, ou, ov, cover):
    du, dv = five[0] - ou, five[1] - ov
    g = du * du + dv * dv + 0.01
    drag = cover * (g * lax.rsqrt(g))
    return drag * du, drag * dv


def sides_kernel(
    pos_ref, tile_ref, near_ref, far_ref, ou_ref, ov_ref, wx_ref, wy_ref, mid_ref, packed_ref, drag_ref, stage, room, *scratch,
):
    s = named(scratch)
    lane = lane_ids()
    grid_rows = ROWS * lax.axis_size("gy")
    edge = edges_x()
    clear_ends(s, BANDS)

    def start(i):
        rows = slice(8 * i, 8 * i + 8)
        east, west = by_parity("gx", near_ref[rows, :], far_ref[rows, :])
        ice = yield from ice_strips(chunk_of(tile_ref, i), west, east, edge, lane)
        put_ice(s, i, ice, at_row(i), grid_rows)
        half, j = divmod(i, BANDS // 2)
        sea = slice(ROWS + 8 * j, ROWS + 8 * j + 8)
        own = [ref[rows, :] for ref in (ou_ref, ov_ref, wx_ref, wy_ref)]
        east, west = by_parity("gx", near_ref[sea, :], far_ref[sea, :])
        put_ocean(s, i, (yield from ocean_strips(own, west, east, half, lane)))

    interleave([start(i) for i in range(BANDS)], 3)
    run_subcycles(s, range(BANDS), range(BANDS), SUBS)
    refs = (pos_ref, tile_ref, ou_ref, ov_ref, packed_ref)

    def finish(i):
        def mids():
            return [mid_ref[f, 8 * i : 8 * i + 8, :] for f in range(FINAL)]

        drag = drag_ref.at[:, pl.ds(8 * i - HALO, 8), :]
        yield from finish_band(i, mids, lambda: state_of(s, i), refs, drag, stage.at[i], room.at[i], lane)

    interleave([finish(i) for i in range(2, BANDS - 2)], 8)


def stage_scratch(bands):
    return [pltpu.VMEM((bands, 64, LANES), F32), pltpu.VMEM((bands, 2, 4, 8, LANES), F32)]


def results(rows):
    return pltpu.VMEM((2 * TILES * 2 * FINAL, LANES), F32), jax.ShapeDtypeStruct((2, rows, LANES), F32)


def sides(pos, tile, west, east, ocean, mid):
    return pl.pallas_call(
        sides_kernel,
        in_specs=specs(9),
        out_shape=results(ROWS - 2 * HALO),
        out_specs=specs(3)[1:],
        scratch_shapes=stage_scratch(BANDS) + state_scratch(BANDS),
        compiler_params=pltpu.CompilerParams(vmem_limit_bytes=VMEM_BYTES),
        cost_estimate=pl.CostEstimate(flops=5_000_000, bytes_accessed=5_000_000, transcendentals=800_000),
        name="sides",
    )(pos, tile, west, east, *ocean, mid)


def ends_kernel(
    pos_ref, tile_ref, near_ref, far_ref, inner_ref, outer_ref, ou_ref, ov_ref, wx_ref, wy_ref,
    packed_in, packed_ref, drag_ref, stage, room, *scratch,
):
    del packed_in
    s = named(scratch)
    lane = lane_ids()
    grid_rows = ROWS * lax.axis_size("gy")
    edge = edges_x()
    outside = edges_y()
    ocean_refs = (ou_ref, ov_ref, wx_ref, wy_ref)
    clear_ends(s, 24)

    def start(end, j):
        i = (j - 2) if end == 0 else BANDS - 4 + j
        half = 1 - end if not 0 <= i < BANDS else i // (BANDS // 2)
        if 0 <= i < BANDS:
            rows = slice(8 * i, 8 * i + 8)
            own = chunk_of(tile_ref, i)
            east, west = by_parity("gx", near_ref[rows, :], far_ref[rows, :])
            water = [x[rows, :] for x in ocean_refs]
            at = ROWS + 8 * (i % (BANDS // 2))
            sea_east, sea_west = by_parity("gx", near_ref[at : at + 8, :], far_ref[at : at + 8, :])
        else:
            at = 8 * (i % 2)

            def part_of(base):
                rows = slice(base, base + 8)
                south, north = by_parity("gy", inner_ref[rows, :], outer_ref[rows, :])
                return south if end else north

            own = [jnp.where(outside[end], 0.0, part_of(i % 2 * 64 + 8 * f)) for f in range(FIELDS)]
            east, west = by_parity("gx", part_of(128 + at), part_of(144 + at))
            west, east = jnp.where(outside[end], 0.0, west), jnp.where(outside[end], 0.0, east)
            water = [part_of(160 + 16 * f + at) for f in range(4)]
            sea_east, sea_west = by_parity("gx", part_of(224 + at), part_of(240 + at))
        for part in range(2):
            chunk = part * 12 + end * 6 + j
            ice = (yield from ice_strips(own, west, east, edge, lane)) if part else own
            put_ice(s, chunk, ice, at_row(i), grid_rows)
            if part:
                water = yield from ocean_strips(water, sea_west, sea_east, half, lane)
            put_ocean(s, chunk, water)

    interleave([start(end, j) for end in range(2) for j in range(6)], 3)
    every = range(24)
    four = [c for c in every if c % 6 not in (0, 5)]
    two = [c for c in every if c % 6 in (2, 3)]
    for step in range(1, SUBS + 1):
        stress = every if step < 5 else four
        run_subcycles(s, stress, every if step < 4 else four if step < 8 else two)
    refs = (pos_ref, tile_ref, ou_ref, ov_ref, packed_ref)

    def finish(n):
        end, j = divmod(n, 2)
        chunk = end * 6 + j + 2
        i = BANDS - 2 + j if end else j
        drag = drag_ref.at[:, pl.ds(8 * n, 8), :]
        yield from finish_band(i, lambda: state_of(s, chunk), lambda: state_of(s, chunk + 12), refs, drag, stage.at[n], room.at[n], lane)

    interleave([finish(n) for n in range(4)], 4)


def ends(pos, tile, west, east, north, south, ocean, packed):
    packed = pltpu.with_memory_space_constraint(packed, pltpu.VMEM)
    return pl.pallas_call(
        ends_kernel,
        in_specs=specs(11),
        out_shape=results(2 * HALO),
        out_specs=specs(3)[1:],
        input_output_aliases={10: 0},
        scratch_shapes=stage_scratch(4) + state_scratch(24),
        compiler_params=pltpu.CompilerParams(vmem_limit_bytes=VMEM_BYTES),
        name="ends",
    )(pos, tile, west, east, north, south, *ocean, packed)


def unpack_ice_kernel(starts_ref, recv_ref, mid_ref, end_ref, vel_out, str_out, drag_out, blk, vel_ref, str_ref, sems):
    first, last = pl.ds(0, HALO), pl.ds(ROWS - HALO, HALO)
    copies = [
        pltpu.make_async_copy(mid_ref, drag_out.at[:, pl.ds(HALO, ROWS - 2 * HALO), :], sems.at[0]),
        pltpu.make_async_copy(end_ref.at[:, first, :], drag_out.at[:, first, :], sems.at[1]),
        pltpu.make_async_copy(end_ref.at[:, pl.ds(HALO, HALO), :], drag_out.at[:, last, :], sems.at[2]),
    ]
    for copy in copies:
        copy.start()
    for t in range(TILES):
        start = starts_ref[0, t]
        for c in range(2):
            at = (2 * t + c) * 2 * FINAL
            to = pl.multiple_of((start + c) * 16, 16)
            blk[pl.ds(to, 2 * FINAL), :] = recv_ref[at : at + 2 * FINAL, :]
    half = SLOTS // 2
    for part in range(2):
        for g in range(part * half // 8, (part + 1) * half // 8):
            eight = slice(8 * g, 8 * g + 8)
            for h in range(2):
                cut = slice(h * LANES, (h + 1) * LANES)
                for f in range(3):
                    str_ref[f, eight, cut] = blk[pl.ds(128 * g + h * FINAL + 2 + f, 8, stride=16), :]
                for j in range(8):
                    at = 128 * g + 16 * j + h * FINAL
                    vel_ref[8 * g + j, :, cut] = blk[at : at + 2, :]
        some = pl.ds(part * half, half)
        parts = [
            pltpu.make_async_copy(vel_ref.at[some], vel_out.at[some], sems.at[3 + 2 * part]),
            pltpu.make_async_copy(str_ref.at[:, some, :], str_out.at[:, some, :], sems.at[4 + 2 * part]),
        ]
        for copy in parts:
            copy.start()
        copies += parts
    for copy in copies:
        copy.wait()


def unpack_ice(starts, recv, drag_mid, drag_ends):
    vel_shape, str_shape = (SLOTS, 2, 2 * LANES), (3, SLOTS, 2 * LANES)
    vel, strs, drag = pl.pallas_call(
        unpack_ice_kernel,
        in_specs=specs(4),
        out_specs=[pl.BlockSpec(memory_space=pltpu.HBM)] * 3,
        out_shape=tuple(pltpu.HBM(shape, F32) for shape in (vel_shape, str_shape, (2, ROWS, LANES))),
        scratch_shapes=[
            pltpu.VMEM(((SLOTS + 8) * 16, LANES), F32),
            pltpu.VMEM(vel_shape, F32),
            pltpu.VMEM(str_shape, F32),
            pltpu.SemaphoreType.DMA((7,)),
        ],
        compiler_params=pltpu.CompilerParams(vmem_limit_bytes=VMEM_BYTES),
        name="unpack_ice",
    )(starts, recv, drag_mid, drag_ends)
    return vel, jnp.transpose(strs, (1, 0, 2)), drag


def exchange(axis, near, far):
    nx, ny = lax.axis_size("gx"), lax.axis_size("gy")
    swaps = ([], [])
    for a in range(nx):
        for b in range(ny):
            at, n = (a, nx) if axis == "gx" else (b, ny)
            for swap, step in zip(swaps, (1 - at % 2 * 2, at % 2 * 2 - 1)):
                to = (a + step, b) if axis == "gx" else (a, b + step)
                if not 0 <= at + step < n:
                    to = (a, b ^ 1) if axis == "gx" else (a ^ 1, b)
                swap.append((a * ny + b, to[0] * ny + to[1]))
    far = lax.ppermute(far, AXES, swaps[1])
    return lax.ppermute(near, AXES, swaps[0]), far


def on_device(
    owner_list, ice_mask, velocity, stress, thickness, concentration, ocean_u, ocean_v, wind_x, wind_y, surface_temp
):
    ocean = (ocean_u, ocean_v, wind_x, wind_y)
    outbound, starts, pos, sea_west, sea_east, *maps = pack(
        owner_list, ice_mask, velocity, stress, thickness, concentration, (*ocean, surface_temp)
    )
    *ocean, surface_temp = maps
    arrived = lax.all_to_all(outbound, AXES, split_axis=0, concat_axis=0, tiled=True)
    tile, near, far, even = unpack_tile(pos, arrived, surface_temp, sea_west, sea_east)
    near, far = exchange("gx", near, far)
    near, far, mid, *ocean = lax.optimization_barrier((near, far, inner(tile, ocean), *ocean))

    def edge(cells, block_rows, sea_rows):
        parts = [tile[block_rows], near[:ROWS][cells], far[:ROWS][cells]]
        parts += [x[cells] for x in ocean] + [near[sea_rows], far[sea_rows]]
        return jnp.concatenate(parts, axis=0)

    low = edge(slice(0, HALO), slice(0, 128), slice(ROWS, ROWS + HALO))
    high = edge(slice(ROWS - HALO, ROWS), slice(-128, None), slice(EDGE - HALO, EDGE))
    even = even[:1] > 0.5
    near_y, far_y = exchange("gy", jnp.where(even, high, low), jnp.where(even, low, high))
    packed, drag_mid = sides(pos, tile, near, far, ocean, mid)
    packed, drag_ends = ends(pos, tile, near, far, near_y, far_y, ocean, packed)

    homeward = packed.reshape(2 * TILES, FINAL, 2, LANES)
    back = lax.all_to_all(homeward, AXES, split_axis=0, concat_axis=0, tiled=True)
    return unpack_ice(starts, back.reshape(2 * TILES * 2 * FINAL, LANES), drag_mid, drag_ends)


def solution(mesh):
    blocks = P(AXES, None, None)
    return jax.shard_map(
        on_device,
        mesh=mesh,
        in_specs=(P(), P(AXES, None)) + (blocks,) * 4 + (P("gy", "gx"),) * 5,
        out_specs=(blocks, blocks, P(None, "gy", "gx")),
        check_vma=False,
    )
```
